32 devices in a mesh: grp: 4 (over z), seq: 8 (over y, x, core).
Axes of the slice: x: 2, y: 2, z: 4, core: 2. Of those that a mesh axis runs over, the one named last changes fastest.
Arguments:
- queries: bfloat16 [16384, 4096], P(('seq', 'grp')), may hold values from -6 to 6
- keys: bfloat16 [16384, 4096], P(('seq', 'grp')), may hold values from -6 to 6
- values: bfloat16 [16384, 4096], P(('seq', 'grp')), may hold values from -6 to 6
- log_decay: float32 [32, 16384], P('grp', 'seq'), may hold values from -1.3 to 0, as said below
- gain: float32 [4096], P('grp'), may hold values from 0.5 to 1.5
Outputs:
- attended: bfloat16 [16384, 4096], P('seq', 'grp')
The draws below stay inside these ranges and needn't reach their ends.
Inputs may be any that keep to these rules, and one draw needn't show every extreme that they name: log_decay is negative everywhere.
All inputs are finite; a program needn't handle non-finite values.
Results may differ from the reference program's by a relative error of at most 0.0059.
Values may be sent and summed in bfloat16 or wider, within the bound.
No kernel may reach another device: no remote copies, remote signals or barrier semaphores. Data moves between devices by JAX's collectives and lax.ppermute only.
A program may use at most 128 MiB of HBM per device.

```python
import math
import jax
import jax.numpy as jnp
from jax import lax

HEAD_TOTAL = 32
HEAD_DIM = 128
T_DEV = 2048
TOKEN_TOTAL = 16384


def draw_log_decay(key, part):
    every_key = jax.random.split(jax.random.fold_in(key, 17), 6)
    block_count = TOKEN_TOTAL // T_DEV
    slow_share = 0.5
    slow_heads = jax.random.uniform(every_key[0], (HEAD_TOTAL, 1)) < slow_share
    slow_rates = jnp.exp(jax.random.uniform(every_key[1], (HEAD_TOTAL, 1), minval=math.log(0.1), maxval=math.log(0.5))) / TOKEN_TOTAL
    fast_rates = jnp.exp(jax.random.uniform(every_key[2], (HEAD_TOTAL, 1), minval=math.log(1.0 / 50.0), maxval=math.log(1.0 / 30.0)))
    base_rates = jnp.where(slow_heads, slow_rates, fast_rates)
    factor = jnp.exp(jax.random.uniform(every_key[3], (HEAD_TOTAL, block_count), minval=math.log(0.5), maxval=math.log(2.0)))
    rates = base_rates * jnp.repeat(factor, T_DEV, axis=1)
    spike_location = jax.random.randint(every_key[4], (3,), 0, TOKEN_TOTAL)
    spike_penalty = jax.random.uniform(every_key[5], (HEAD_TOTAL, 3), minval=0.2, maxval=0.33)
    position_index = jnp.arange(TOKEN_TOTAL)
    final_output = -rates
    for selected_index in range(3):
        spike_mask = (position_index == spike_location[selected_index]).astype(jnp.float32)
        final_output = final_output + jnp.log1p(-spike_penalty[:, selected_index:selected_index + 1]) * spike_mask[None, :]
    return final_output.astype(jnp.float32)


def level_of(own_key, dims, shards, least, largest):
    factor_of, own = 1.0, jax.random.fold_in(own_key, 6)
    for dim, blocks in shards:
        steps = jnp.exp(jax.random.uniform(jax.random.fold_in(own, dim), (blocks,), jnp.float32, least / len(shards), largest / len(shards)))
        factor_of = factor_of * jnp.repeat(steps, dims[dim] // blocks).reshape([-1 if axis == dim else 1 for axis in range(len(dims))])
    return factor_of


def gaussian(stream_key, extent, width, limit, shards=(), held_as=jnp.bfloat16):
    drawn = jax.random.normal(stream_key, extent, jnp.float32) * width
    if len(shards) > 0:
        drawn = level_of(stream_key, extent, shards, -0.22, 0.18) * drawn
    return jnp.clip(drawn, min=-limit, max=limit).astype(held_as)


def setup_inputs(seed: int = 0) -> dict:
    seeds = jax.random.split(jax.random.key(seed), 6)
    return {
        "queries": gaussian(seeds[0], (TOKEN_TOTAL, HEAD_TOTAL * HEAD_DIM), 1.0, 6.0, ((0, 32),)),
        "keys": gaussian(seeds[1], (TOKEN_TOTAL, HEAD_TOTAL * HEAD_DIM), 1.0, 6.0, ((0, 32),)),
        "values": gaussian(seeds[2], (TOKEN_TOTAL, HEAD_TOTAL * HEAD_DIM), 1.0, 6.0, ((0, 32),)),
        "log_decay": draw_log_decay(jax.random.fold_in(seeds[5], 71), 0),
        "gain": jnp.clip(1.0 + 0.1 * jax.random.normal(seeds[4], (HEAD_TOTAL * HEAD_DIM,), jnp.float32), 0.5, 1.5),
    }


def local_mix(query_part, key_part, value_part, levels):
    highest = lax.Precision.HIGHEST
    row_total = query_part.shape[0]
    block_rows = min(512, row_total)
    pieces = []
    for start in range(0, row_total, block_rows):
        finish = start + block_rows
        scores = jnp.einsum('thd,shd->hts', query_part[start:finish], key_part[:finish], precision=highest)
        causal = jnp.arange(start, finish, dtype=jnp.int32)[:, None] >= jnp.arange(finish, dtype=jnp.int32)[None, :]
        decay_gap = jnp.where(causal[None], levels[:, start:finish, None] - levels[:, None, :finish], 0.0)
        weights = jnp.where(causal[None], scores * jnp.exp(decay_gap), 0.0).astype(jnp.bfloat16)
        weights = lax.optimization_barrier(weights)
        pieces.append(jnp.einsum('hts,shd->thd', weights.astype(jnp.float32), value_part[:finish], precision=highest))
    return jnp.concatenate(pieces, axis=0)

def reference(queries, keys, values, log_decay, gain):
    total_rows = queries.shape[0]
    block_count = total_rows // T_DEV
    query_blocks = queries.reshape(block_count, T_DEV, HEAD_TOTAL, HEAD_DIM)
    key_blocks = keys.reshape(block_count, T_DEV, HEAD_TOTAL, HEAD_DIM)
    value_blocks = values.reshape(block_count, T_DEV, HEAD_TOTAL, HEAD_DIM)
    decay_blocks = log_decay.reshape(HEAD_TOTAL, block_count, T_DEV).transpose(1, 0, 2)
    gain_heads = gain.reshape(HEAD_TOTAL, HEAD_DIM)
    highest = lax.Precision.HIGHEST

    def advance(running_state, inputs):
        query_part, key_part, value_part, decay_part = inputs
        query_wide = query_part.astype(jnp.float32)
        key_wide = key_part.astype(jnp.float32)
        value_wide = value_part.astype(jnp.float32)
        levels = jnp.cumsum(decay_part, axis=1)
        block_total = levels[:, -1]
        local_part = local_mix(query_wide, key_wide, value_wide, levels)
        state_half = lax.optimization_barrier(running_state.astype(jnp.bfloat16))
        scaled_queries = (query_wide * jnp.exp(levels).T[:, :, None]).astype(jnp.bfloat16)
        scaled_queries = lax.optimization_barrier(scaled_queries)
        carried_part = jnp.einsum('thd,hde->the', scaled_queries.astype(jnp.float32), state_half.astype(jnp.float32), precision=highest)
        mixture = local_part + carried_part
        mean_square = lax.optimization_barrier(jnp.mean(mixture * mixture, axis=2, keepdims=True))
        normed = (mixture * lax.rsqrt(mean_square + 1e-06) * gain_heads[None]).astype(jnp.bfloat16)
        tail_decay = jnp.exp(block_total[:, None] - levels)
        scaled_keys = (key_wide * tail_decay.T[:, :, None]).astype(jnp.bfloat16)
        scaled_keys = lax.optimization_barrier(scaled_keys)
        block_state = jnp.einsum('thd,the->hde', scaled_keys.astype(jnp.float32), value_wide, precision=highest)
        next_state = jnp.exp(block_total)[:, None, None] * running_state + block_state
        return (next_state, normed)
    starting = jnp.zeros((HEAD_TOTAL, HEAD_DIM, HEAD_DIM), jnp.float32)
    _, outputs = lax.scan(advance, starting, (query_blocks, key_blocks, value_blocks, decay_blocks))
    return outputs.reshape(total_rows, HEAD_TOTAL * HEAD_DIM)
```

```python
import functools

import jax
import jax.numpy as jnp
from jax import lax
from jax.experimental import pallas as pl
from jax.experimental.pallas import tpu as pltpu
from jax.sharding import PartitionSpec as P

GROUPS = (2, 3, 3)
CHUNK = 256
F32 = jnp.float32
BF16 = jnp.bfloat16


def entering_2(array, axis, combine, identity):
    length, mine = (lax.axis_size(axis), lax.axis_index(axis))
    everything = jax.tree.map(lambda part: lax.all_gather(part, axis), array)
    start = jax.tree.map(
        lambda part, zero: jnp.broadcast_to(jnp.asarray(zero, part.dtype), part.shape),
        array,
        identity,
    )

    def step(k, before):
        reached = k < mine
        new = combine(before, jax.tree.map(lambda part: part[k], everything))
        return jax.tree.map(lambda a, b: jnp.where(reached, a, b), new, before)

    return lax.fori_loop(0, length, step, start)


def local_mix(query_heads, key_heads, value_heads, levels):
    row_total = query_heads.shape[0]
    block_rows = min(512, row_total)
    pieces = []
    for start in range(0, row_total, block_rows):
        finish = start + block_rows
        scores = jnp.einsum(
            "thd,shd->hts",
            query_heads[start:finish],
            key_heads[:finish],
            preferred_element_type=jnp.float32,
        )
        causal = (
            jnp.arange(start, finish, dtype=jnp.int32)[:, None]
            >= jnp.arange(finish, dtype=jnp.int32)[None, :]
        )
        decay_gap = jnp.where(
            causal[None], levels[:, start:finish, None] - levels[:, None, :finish], 0.0
        )
        weights = jnp.where(causal[None], scores * jnp.exp(decay_gap), 0.0).astype(jnp.bfloat16)
        pieces.append(
            jnp.einsum(
                "hts,shd->thd", weights, value_heads[:finish], preferred_element_type=jnp.float32
            )
        )
    return jnp.concatenate(pieces, axis=0)


def local_any(queries, keys, values, log_decay, gain):
    head_count = log_decay.shape[0]
    row_count = log_decay.shape[1]
    head_width = gain.shape[0] // head_count
    query_rows, key_rows, value_rows = (
        lax.all_to_all(queries, "grp", split_axis=1, concat_axis=0, tiled=True),
        lax.all_to_all(keys, "grp", split_axis=1, concat_axis=0, tiled=True),
        lax.all_to_all(values, "grp", split_axis=1, concat_axis=0, tiled=True),
    )
    key_heads = key_rows.reshape(row_count, head_count, head_width)
    value_heads = value_rows.reshape(row_count, head_count, head_width)
    levels = jnp.cumsum(log_decay, axis=1)
    block_total = levels[:, -1]
    tail_decay = jnp.exp(block_total[:, None] - levels)
    scaled_keys = (key_heads.astype(jnp.float32) * tail_decay.T[:, :, None]).astype(jnp.bfloat16)
    block_state = jnp.einsum(
        "thd,the->hde", scaled_keys, value_heads, preferred_element_type=jnp.float32
    )

    def combine_blocks(earlier, later_part):
        return (
            earlier[0] + later_part[0],
            jnp.exp(later_part[0])[:, None, None] * earlier[1] + later_part[1],
        )

    identity = (jnp.zeros_like(block_total), jnp.zeros_like(block_state))
    _, entering = entering_2((block_total, block_state), "seq", combine_blocks, identity)
    query_heads = query_rows.reshape(row_count, head_count, head_width)
    local_part = local_mix(query_heads, key_heads, value_heads, levels)
    state_half = entering.astype(jnp.bfloat16)
    scaled_queries = (query_heads.astype(jnp.float32) * jnp.exp(levels).T[:, :, None]).astype(
        jnp.bfloat16
    )
    carried_part = jnp.einsum(
        "thd,hde->the", scaled_queries, state_half, preferred_element_type=jnp.float32
    )
    mixture = local_part + carried_part
    mean_square = jnp.mean(mixture * mixture, axis=2, keepdims=True)
    normed = mixture * lax.rsqrt(mean_square + 1e-06) * gain.reshape(head_count, head_width)[None]
    return normed.reshape(row_count, head_count * head_width).astype(jnp.bfloat16)


def call(kernel, scalars, arrays, outs, grid=None, in_specs=None, out_specs=None, scratch=(), cost=(0, 0), **kw):
    whole = [pl.BlockSpec(a.shape, lambda *_, n=a.ndim: (0,) * n) for a in arrays]
    whole_out = [pl.BlockSpec(o.shape, lambda *_, n=len(o.shape): (0,) * n) for o in outs]
    return pl.pallas_call(
        kernel,
        out_shape=outs,
        grid_spec=pltpu.PrefetchScalarGridSpec(
            num_scalar_prefetch=1,
            grid=grid or (1,),
            in_specs=in_specs or whole,
            out_specs=out_specs or whole_out,
            scratch_shapes=list(scratch),
        ),
        compiler_params=pltpu.CompilerParams(vmem_limit_bytes=32 * 1024 * 1024),
        cost_estimate=pl.CostEstimate(flops=cost[0], bytes_accessed=cost[1], transcendentals=0),
        **kw,
    )(scalars, *arrays)


def shape(*dims, dtype=BF16):
    return jax.ShapeDtypeStruct(dims, dtype)


def pick(rows, index):
    at = lax.broadcasted_iota(jnp.int32, rows.shape, 0)
    return jnp.sum(jnp.where(at == index, rows, 0.0), axis=0, keepdims=True)


def pack_decays(z_ref, decay_ref, gain_ref, *out_refs):
    z = z_ref[0]
    heads, rows = decay_ref.shape
    parts = len(out_refs)
    width = rows // parts
    lane = lax.broadcasted_iota(jnp.int32, (heads, 128), 1)
    totals = jnp.zeros((heads, 128), F32)
    for c in range(parts):
        total = jnp.sum(decay_ref[:, c * width : (c + 1) * width], axis=1, keepdims=True)
        totals = jnp.where(lane == c, total, totals)
    for k, out_ref in enumerate(out_refs):
        to = lax.rem(z + k, parts)
        out_ref[:, :width] = decay_ref[:, pl.ds(pl.multiple_of(to * width, 128), width)]
        out_ref[:, width : width + 128] = totals
        out_ref[:, width + 128 :] = gain_ref[...]


def unpack_decays(z_ref, *refs):
    parts = len(refs) - 4
    ins, (levels_ref, totals_ref, gains_ref, decays) = refs[:parts], refs[parts:]
    z = z_ref[0]
    heads = ins[0].shape[0]
    width = decays.shape[1]
    for k, in_ref in enumerate(ins):
        home = lax.rem(z + parts - k, parts)
        at = pl.ds(pl.multiple_of(home * heads, heads), heads)
        decays[at, :] = in_ref[:, :width]
        gains_ref[at, :] = in_ref[:, width + 128 :]
        totals = in_ref[:, width : width + 128]
        row = lax.broadcasted_iota(jnp.int32, totals_ref.shape[1:], 0)
        for h in range(heads):
            rows = jnp.zeros(totals_ref.shape[1:], F32)
            for c in range(parts):
                rows = jnp.where(row == c, totals[h : h + 1, c : c + 1], rows)
            totals_ref[home * heads + h] = rows
    upper = lax.broadcasted_iota(jnp.int32, (width, width), 0) <= lax.broadcasted_iota(
        jnp.int32, (width, width), 1
    )
    levels_ref[...] = jnp.dot(
        decays[...],
        jnp.where(upper, 1.0, 0.0).astype(F32),
        precision=lax.Precision.HIGHEST,
        preferred_element_type=F32,
    )


def state_of(key, value, row, end):
    scaled = (key.T.astype(F32) * jnp.exp(end - row)).astype(BF16)
    return jnp.dot(scaled, value, preferred_element_type=F32)


def quarter_states(head_of, z_ref, key_a, value_a, key_b, value_b, levels_ref, keep_ref, send_ref):
    z, i = z_ref[0], pl.program_id(0)
    width = levels_ref.shape[1]
    for other, key, value, out in ((0, key_a, value_a, keep_ref), (1, key_b, value_b, send_ref)):
        row = levels_ref[pl.ds(head_of(i, z, other), 1), :]
        out[0] = state_of(key[...], value[...], row, row[:, width - 1 :]).astype(BF16)


def pair_states(head_of, z_ref, keep_ref, got_ref, totals_ref, out_ref):
    z = z_ref[0]
    odd = lax.rem(z, 2) == 1
    for i in range(keep_ref.shape[0]):
        totals = totals_ref[head_of(i, z, 0)]
        keep, got = keep_ref[i].astype(F32), got_ref[i].astype(F32)
        decay = jnp.exp(pick(totals, 2 * lax.div(z, 2) + 1))
        out_ref[i] = (decay * jnp.where(odd, got, keep) + jnp.where(odd, keep, got)).astype(BF16)


def put_log(ref, i, log):
    high = log.astype(BF16).astype(F32)
    middle = (log - high).astype(BF16).astype(F32)
    low = log - high - middle
    row = lax.broadcasted_iota(jnp.int32, (16, 128), 0)
    rows = jnp.where(row == 0, high, jnp.where(row == 1, middle, jnp.where(row == 2, low, 0.0)))
    ref[i, 128:, :] = rows.astype(BF16)


def get_log(ref, i):
    return jnp.sum(ref[i, 128:, :].astype(F32), axis=0, keepdims=True)


def block_states(head_of, z_ref, pair_ref, got_ref, totals_ref, out_ref):
    z = z_ref[0]
    upper = z >= 2
    for i in range(pair_ref.shape[0]):
        totals = totals_ref[head_of(i, z, 0)]
        mine, got = pair_ref[i].astype(F32), got_ref[i].astype(F32)
        decay = jnp.exp(pick(totals, 2) + pick(totals, 3))
        state = decay * jnp.where(upper, got, mine) + jnp.where(upper, mine, got)
        out_ref[i, :128, :] = state.astype(BF16)
        put_log(out_ref, i, jnp.sum(totals, axis=0, keepdims=True))


def scan_step(bit, s_ref, i, own_ref, got_ref, before, before_log):
    upper = (s_ref[1] >> bit) & 1 == 1
    own, got = own_ref[i, :128, :].astype(F32), got_ref[i, :128, :].astype(F32)
    own_log, got_log = get_log(own_ref, i), get_log(got_ref, i)
    if before is None:
        after = jnp.where(upper, got, 0.0)
        after_log = jnp.where(upper, got_log, 0.0)
    else:
        after = jnp.where(upper, jnp.exp(before_log) * got + before, before)
        after_log = jnp.where(upper, before_log + got_log, before_log)
    total = jnp.exp(jnp.where(upper, own_log, got_log)) * jnp.where(upper, got, own) + jnp.where(upper, own, got)
    return after, after_log, total, own_log + got_log


def scan_blocks(bit, s_ref, own_ref, got_ref, *refs):
    before_ref = refs[0] if bit else None
    after_ref, total_ref = refs[-2:]
    for i in range(own_ref.shape[0]):
        before = before_ref[i, :128, :] if bit else None
        before_log = before_ref[i, 128:129, :] if bit else None
        after, after_log, total, total_log = scan_step(bit, s_ref, i, own_ref, got_ref, before, before_log)
        after_ref[i, :128, :] = after
        after_ref[i, 128:, :] = jnp.broadcast_to(after_log, (8, 128))
        total_ref[i, :128, :] = total.astype(BF16)
        put_log(total_ref, i, total_log)


def entering_states(head_of, bit, s_ref, own_ref, got_ref, before_ref, keep_ref, keep_got_ref, low_ref, totals_ref, out_ref, send_ref):
    z = s_ref[0]
    odd, upper = lax.rem(z, 2) == 1, z >= 2
    for i in range(own_ref.shape[0]):
        totals = totals_ref[head_of(i, z, 0)]
        state = scan_step(
            bit, s_ref, i, own_ref, got_ref, before_ref[i, :128, :], before_ref[i, 128:129, :]
        )[0]
        first, second = pick(totals, 0), pick(totals, 1)
        even_state = jnp.where(
            upper, jnp.exp(first + second) * state + low_ref[i].astype(F32), state
        )
        even_part = jnp.where(odd, keep_got_ref[i], keep_ref[i]).astype(F32)
        decay = jnp.exp(jnp.where(upper, pick(totals, 2), first))
        odd_state = decay * even_state + even_part
        out_ref[i] = jnp.where(odd, odd_state, even_state).astype(BF16)
        send_ref[i] = jnp.where(odd, even_state, odd_state).astype(BF16)


def mix_head(query, key, value, row, entering, gain):
    rows = query.shape[0]
    chunk = min(CHUNK, rows)
    column = jnp.broadcast_to(row, (128, rows)).T
    causal = lax.broadcasted_iota(jnp.int32, (chunk, chunk), 0) >= lax.broadcasted_iota(
        jnp.int32, (chunk, chunk), 1
    )
    state = entering.astype(F32)
    start_level = jnp.zeros((1, 1), F32)
    pieces = []
    for start in range(0, rows, chunk):
        stop = start + chunk
        q, k, v = query[start:stop], key[start:stop], value[start:stop]
        r, c = row[:, start:stop], column[start:stop]
        scores = lax.dot_general(q, k, (((1,), (1,)), ((), ())), preferred_element_type=F32)
        gap = jnp.where(causal, jnp.concatenate([c] * (chunk // 128), axis=1) - r, -1e30)
        weights = (scores * jnp.exp(gap)).astype(BF16)
        scaled = (q.astype(F32) * jnp.exp(c - start_level)).astype(BF16)
        mixture = jnp.dot(weights, v, preferred_element_type=F32) + jnp.dot(
            scaled, state.astype(BF16), preferred_element_type=F32
        )
        mean_square = jnp.mean(mixture * mixture, axis=1, keepdims=True)
        pieces.append((mixture * lax.rsqrt(mean_square + 1e-6) * gain).astype(BF16))
        if stop < rows:
            end = row[:, stop - 1 : stop]
            state = jnp.exp(end - start_level) * state + state_of(k, v, r, end)
            start_level = end
    return pieces


def attend(first, parts, heads, z_ref, *refs):
    ins, outs = refs[: 4 * parts + 2], refs[4 * parts + 2 :]
    levels_ref, gains_ref = ins[-2:]
    for k in range(parts):
        query, key, value, state = ins[4 * k : 4 * k + 4]
        head = lax.rem(z_ref[0] + k, parts) * heads + first + pl.program_id(0)
        pieces = mix_head(
            query[...], key[...], value[...], levels_ref[pl.ds(head, 1), :], state[0], gains_ref[pl.ds(head, 1), :]
        )
        size = pieces[0].shape[0]
        for n, piece in enumerate(pieces):
            outs[k][n * size : (n + 1) * size, :] = piece


def place(first, parts, with_alias, z_ref, *refs):
    pieces, out_ref, sems = refs[:parts], refs[-2], refs[-1]
    rows, width = pieces[0].shape
    copies = []
    for k in range(parts):
        source = lax.rem(z_ref[0] + parts - k, parts)
        copies.append(
            pltpu.make_async_copy(
                pieces[k],
                out_ref.at[pl.ds(pl.multiple_of(source * rows, rows), rows), pl.ds(first * 128, width)],
                sems.at[k],
            )
        )
    for copy in copies:
        copy.start()
    for copy in copies:
        copy.wait()


def local(queries, keys, values, log_decay, gain):
    heads, block = log_decay.shape
    parts = lax.axis_size("grp")
    blocks = lax.axis_size("seq")
    rows, columns = queries.shape
    z, b = lax.axis_index("grp"), lax.axis_index("seq")
    scalars = jnp.stack([z, b]).astype(jnp.int32)

    def shift(x, k):
        return lax.ppermute(x, "grp", [(i, (i + k) % parts) for i in range(parts)])

    def swap(x, axis, bit):
        return lax.ppermute(x, axis, [(i, i ^ bit) for i in range(lax.axis_size(axis))])

    packed = call(
        pack_decays, scalars, [log_decay, gain.reshape(heads, 128)],
        [shape(heads, rows + 256, dtype=F32)] * parts,
    )
    got = [packed[0]] + [shift(packed[k], k) for k in range(1, parts)]
    levels, totals, gains = call(
        unpack_decays, scalars, got,
        [shape(heads * parts, rows, dtype=F32), shape(heads * parts, 8, 128, dtype=F32), shape(heads * parts, 128, dtype=F32)],
        scratch=[pltpu.VMEM((heads * parts, rows), F32)],
    )
    whole = lambda a: pl.BlockSpec(a.shape, lambda *_: (0,) * a.ndim)

    starts = [sum(GROUPS[:g]) for g in range(len(GROUPS))]
    pieces = []
    for first, m in zip(starts, GROUPS):
        n = 2 * m

        def head_of(i, z, other, first=first, m=m):
            home = 2 * (i // m) + lax.rem(z + other, 2)
            return home * heads + first + i % m

        def head_of_dyn(i, z, other, first=first, m=m):
            home = 2 * lax.div(i, m) + lax.rem(z + other, 2)
            return home * heads + first + lax.rem(i, m)

        def column(other):
            return pl.BlockSpec((rows, 128), lambda i, s: (0, head_of_dyn(i, s[0], other)))

        one = pl.BlockSpec((1, 128, 128), lambda i, s: (i, 0, 0))
        keep, send = call(
            functools.partial(quarter_states, head_of_dyn), scalars, [keys, values, keys, values, levels],
            [shape(n, 128, 128)] * 2,
            grid=(n,),
            in_specs=[column(0), column(0), column(1), column(1), whole(levels)],
            out_specs=[one, one],
            cost=(4 * n * rows * 128 * 128, 4 * n * rows * 256),
        )
        got = swap(send, "grp", 1)
        pair, = call(functools.partial(pair_states, head_of), scalars, [keep, got, totals], [shape(n, 128, 128)])
        pair_got = swap(pair, "grp", 2)
        total, = call(functools.partial(block_states, head_of), scalars, [pair, pair_got, totals], [shape(n, 144, 128)])
        before = []
        bits = blocks.bit_length() - 1
        for bit in range(bits - 1):
            other = swap(total, "seq", 1 << bit)
            after, total = call(
                functools.partial(scan_blocks, bit), scalars, [total, other, *before],
                [shape(n, 136, 128, dtype=F32), shape(n, 144, 128)],
            )
            before = [after]
        other = swap(total, "seq", 1 << (bits - 1))
        own, send = call(
            functools.partial(entering_states, head_of, bits - 1), scalars,
            [total, other, *before, keep, got, pair_got, totals],
            [shape(n, 128, 128)] * 2,
        )
        states = [own, swap(send, "grp", 1)]

        arrays, specs = [], []
        for k in range(parts):
            spec = pl.BlockSpec(
                (rows, 128), lambda j, s, k=k, first=first: (0, lax.rem(s[0] + k, parts) * heads + first + j)
            )
            arrays += [queries, keys, values, states[k % 2]]
            specs += [spec] * 3 + [
                pl.BlockSpec((1, 128, 128), lambda j, s, k=k, m=m: (lax.div(lax.rem(s[0] + k, parts), 2) * m + j, 0, 0))
            ]
        outs = call(
            functools.partial(attend, first, parts, heads), scalars, [*arrays, levels, gains],
            [shape(rows, m * 128)] * parts,
            grid=(m,),
            in_specs=[*specs, whole(levels), whole(gains)],
            out_specs=[pl.BlockSpec((rows, 128), lambda j, s: (0, j))] * parts,
            cost=(parts * m * 4 * rows * 128 * 512, parts * m * rows * 1024),
        )
        pieces.append([outs[0]] + [shift(outs[k], k) for k in range(1, parts)])

    out = None
    for first, group in zip(starts, pieces):
        alias = [] if out is None else [out]
        any_spec = pl.BlockSpec(memory_space=pl.ANY)
        out, = call(
            functools.partial(place, first, parts, bool(alias)), scalars, [*group, *alias],
            [shape(block, heads * 128)],
            in_specs=[any_spec] * (parts + len(alias)),
            out_specs=[any_spec],
            scratch=[pltpu.SemaphoreType.DMA((parts,))],
            input_output_aliases={parts + 1: 0} if alias else {},
        )
    return out


def solution(mesh):
    parts, blocks = mesh.shape["grp"], mesh.shape["seq"]
    fits = parts == 4 and blocks >= 4 and blocks & (blocks - 1) == 0
    in_specs = (
        P(("seq", "grp"), None),
        P(("seq", "grp"), None),
        P(("seq", "grp"), None),
        P("grp", "seq"),
        P("grp"),
    )
    out_specs = P("seq", "grp")
    return jax.shard_map(
        local if fits else local_any, mesh=mesh, in_specs=in_specs, out_specs=out_specs, check_vma=False
    )
```

```python
import functools

import jax
import jax.numpy as jnp
from jax import lax
from jax.experimental import pallas as pl
from jax.experimental.pallas import tpu as pltpu
from jax.sharding import PartitionSpec as P

GROUPS = ((3, 0, (1, 2)), (5, 0, (1, 2, 2)))
ORDER = ('k0', 'k1', 'k0', 'k0', 'k1', 'k0', 'k0', 'k1', 'k0', 'k1', 'k0', 'w001', 'k1', 'w003', 'k0', 'w002', 'k1', 'w011', 'k1', 'w012', 'k1', 'w013', 'w101', 'k1', 'p00', 'p01', 'p10', 'p11', 'p12')
CHUNK = 256
VMEM_BYTES = 16 * 1024 * 1024
SCALE = 1.0e9
STREAM_VMEM_BYTES = 16 * 1024 * 1024
F32 = jnp.float32
BF16 = jnp.bfloat16


def entering_2(array, axis, combine, identity):
    length, mine = (lax.axis_size(axis), lax.axis_index(axis))
    everything = jax.tree.map(lambda part: lax.all_gather(part, axis), array)
    start = jax.tree.map(
        lambda part, zero: jnp.broadcast_to(jnp.asarray(zero, part.dtype), part.shape),
        array,
        identity,
    )

    def step(k, before):
        reached = k < mine
        new = combine(before, jax.tree.map(lambda part: part[k], everything))
        return jax.tree.map(lambda a, b: jnp.where(reached, a, b), new, before)

    return lax.fori_loop(0, length, step, start)


def local_mix(query_heads, key_heads, value_heads, levels):
    row_total = query_heads.shape[0]
    block_rows = min(512, row_total)
    pieces = []
    for start in range(0, row_total, block_rows):
        finish = start + block_rows
        scores = jnp.einsum(
            "thd,shd->hts",
            query_heads[start:finish],
            key_heads[:finish],
            preferred_element_type=jnp.float32,
        )
        causal = (
            jnp.arange(start, finish, dtype=jnp.int32)[:, None]
            >= jnp.arange(finish, dtype=jnp.int32)[None, :]
        )
        decay_gap = jnp.where(
            causal[None], levels[:, start:finish, None] - levels[:, None, :finish], 0.0
        )
        weights = jnp.where(causal[None], scores * jnp.exp(decay_gap), 0.0).astype(jnp.bfloat16)
        pieces.append(
            jnp.einsum(
                "hts,shd->thd", weights, value_heads[:finish], preferred_element_type=jnp.float32
            )
        )
    return jnp.concatenate(pieces, axis=0)


def local_any(queries, keys, values, log_decay, gain):
    head_count = log_decay.shape[0]
    row_count = log_decay.shape[1]
    head_width = gain.shape[0] // head_count
    query_rows, key_rows, value_rows = (
        lax.all_to_all(queries, "grp", split_axis=1, concat_axis=0, tiled=True),
        lax.all_to_all(keys, "grp", split_axis=1, concat_axis=0, tiled=True),
        lax.all_to_all(values, "grp", split_axis=1, concat_axis=0, tiled=True),
    )
    key_heads = key_rows.reshape(row_count, head_count, head_width)
    value_heads = value_rows.reshape(row_count, head_count, head_width)
    levels = jnp.cumsum(log_decay, axis=1)
    block_total = levels[:, -1]
    tail_decay = jnp.exp(block_total[:, None] - levels)
    scaled_keys = (key_heads.astype(jnp.float32) * tail_decay.T[:, :, None]).astype(jnp.bfloat16)
    block_state = jnp.einsum(
        "thd,the->hde", scaled_keys, value_heads, preferred_element_type=jnp.float32
    )

    def combine_blocks(earlier, later_part):
        return (
            earlier[0] + later_part[0],
            jnp.exp(later_part[0])[:, None, None] * earlier[1] + later_part[1],
        )

    identity = (jnp.zeros_like(block_total), jnp.zeros_like(block_state))
    _, entering = entering_2((block_total, block_state), "seq", combine_blocks, identity)
    query_heads = query_rows.reshape(row_count, head_count, head_width)
    local_part = local_mix(query_heads, key_heads, value_heads, levels)
    state_half = entering.astype(jnp.bfloat16)
    scaled_queries = (query_heads.astype(jnp.float32) * jnp.exp(levels).T[:, :, None]).astype(
        jnp.bfloat16
    )
    carried_part = jnp.einsum(
        "thd,hde->the", scaled_queries, state_half, preferred_element_type=jnp.float32
    )
    mixture = local_part + carried_part
    mean_square = jnp.mean(mixture * mixture, axis=2, keepdims=True)
    normed = mixture * lax.rsqrt(mean_square + 1e-06) * gain.reshape(head_count, head_width)[None]
    return normed.reshape(row_count, head_count * head_width).astype(jnp.bfloat16)


def in_vmem():
    return pl.BlockSpec(memory_space=pltpu.VMEM)


def anywhere():
    return pl.BlockSpec(memory_space=pl.ANY)


class Calls:
    def __init__(self, scalars):
        self.scalars, self.after = scalars, []

    def __call__(self, kernel, arrays, outs, streams=(), out_specs=None, scratch=(), cost=1000, aliases=None):
        count = len(arrays) + len(streams)
        after, self.after = [a for a in self.after if not any(a is b for b in arrays)], []

        def body(s_ref, *refs):
            kernel(s_ref, *refs[:count], *refs[count + len(after) :])

        results = pl.pallas_call(
            body,
            out_shape=outs,
            in_specs=[
                pl.BlockSpec(memory_space=pltpu.SMEM),
                *[anywhere() if aliases and n in aliases else in_vmem() for n in range(len(arrays))],
                *[pl.BlockSpec(memory_space=pltpu.HBM)] * len(streams),
                *[anywhere()] * len(after),
            ],
            out_specs=out_specs or [in_vmem()] * len(outs),
            scratch_shapes=list(scratch),
            compiler_params=pltpu.CompilerParams(vmem_limit_bytes=STREAM_VMEM_BYTES if streams else VMEM_BYTES),
            cost_estimate=pl.CostEstimate(flops=cost, bytes_accessed=1000, transcendentals=0),
            input_output_aliases={n + 1: o for n, o in (aliases or {}).items()},
        )(self.scalars, *arrays, *streams, *after)
        self.after.append(results[0])
        return results


def cost_us(time):
    return int(time * SCALE)


def shape(*dims, dtype=BF16):
    return jax.ShapeDtypeStruct(dims, dtype)


def pick(rows, index):
    at = lax.broadcasted_iota(jnp.int32, rows.shape, 0)
    return jnp.sum(jnp.where(at == index, rows, 0.0), axis=0, keepdims=True)


def pack_decays(s_ref, decay_ref, gain_ref, *out_refs):
    z = s_ref[0]
    heads, rows = decay_ref.shape
    parts = len(out_refs)
    width = rows // parts
    lane = lax.broadcasted_iota(jnp.int32, (heads, 128), 1)
    totals = jnp.zeros((heads, 128), F32)
    for c in range(parts):
        total = jnp.sum(decay_ref[:, c * width : (c + 1) * width], axis=1, keepdims=True)
        totals = jnp.where(lane == c, total, totals)
    for k, out_ref in enumerate(out_refs):
        to = lax.rem(z + k, parts)
        out_ref[:, :width] = decay_ref[:, pl.ds(pl.multiple_of(to * width, 128), width)]
        out_ref[:, width : width + 128] = totals
        out_ref[:, width + 128 :] = gain_ref[...]


def unpack_decays(z_ref, *refs):
    parts = len(refs) - 4
    ins, (levels_ref, totals_ref, gains_ref, decays) = refs[:parts], refs[parts:]
    z = z_ref[0]
    heads = ins[0].shape[0]
    width = decays.shape[1]
    for k, in_ref in enumerate(ins):
        home = lax.rem(z + parts - k, parts)
        at = pl.ds(pl.multiple_of(home * heads, heads), heads)
        decays[at, :] = in_ref[:, :width]
        gains_ref[at, :] = in_ref[:, width + 128 :]
        totals = in_ref[:, width : width + 128]
        row = lax.broadcasted_iota(jnp.int32, totals_ref.shape[1:], 0)
        for h in range(heads):
            rows = jnp.zeros(totals_ref.shape[1:], F32)
            for c in range(parts):
                rows = jnp.where(row == c, totals[h : h + 1, c : c + 1], rows)
            totals_ref[home * heads + h] = rows
    upper = lax.broadcasted_iota(jnp.int32, (width, width), 0) <= lax.broadcasted_iota(
        jnp.int32, (width, width), 1
    )
    levels_ref[...] = jnp.dot(
        decays[...],
        jnp.where(upper, 1.0, 0.0).astype(F32),
        precision=lax.Precision.HIGHEST,
        preferred_element_type=F32,
    )


def put_log(ref, i, log):
    high = log.astype(BF16).astype(F32)
    middle = (log - high).astype(BF16).astype(F32)
    low = log - high - middle
    row = lax.broadcasted_iota(jnp.int32, (16, 128), 0)
    rows = jnp.where(row == 0, high, jnp.where(row == 1, middle, jnp.where(row == 2, low, 0.0)))
    ref[(*i, pl.ds(ref.shape[-2] - 16, 16))] = rows.astype(BF16)


def get_log(ref, i):
    return jnp.sum(ref[(*i, pl.ds(ref.shape[-2] - 16, 16))].astype(F32), axis=0, keepdims=True)


def state_of(key, value, row, end):
    scaled = (key.T.astype(F32) * jnp.exp(end - row)).astype(BF16)
    return jnp.dot(scaled, value, preferred_element_type=F32)


def half_states(first, heads, s_ref, levels_ref, keys_ref, values_ref, keep_ref, send_ref):
    z = s_ref[0]
    m = keep_ref.shape[0] // 2
    rows = levels_ref.shape[1]
    places = [(out, n, 2 * n + lax.rem(z + other, 2)) for other, out in enumerate((keep_ref, send_ref)) for n in range(2)]

    def step(*refs):
        j = pl.program_id(0)
        for k, (out, n, home) in enumerate(places):
            row = levels_ref[pl.ds(home * heads + first + j, 1), :]
            state = state_of(refs[2 * k][...], refs[2 * k + 1][...], row, row[:, rows - 1 :])
            out[n * m + j] = state.astype(BF16)

    specs = [pl.BlockSpec((rows, 128), lambda j, home=home: (0, home * heads + first + j)) for _, _, home in places]
    pltpu.emit_pipeline(step, grid=(m,), in_specs=[spec for spec in specs for _ in range(2)])(
        *[keys_ref, values_ref] * len(places)
    )


def pair_states(head_of, z_ref, keep_ref, got_ref, totals_ref, out_ref):
    z = z_ref[0]
    odd = lax.rem(z, 2) == 1
    for i in range(keep_ref.shape[0]):
        totals = totals_ref[head_of(i, z, 0)]
        keep, got = keep_ref[i].astype(F32), got_ref[i].astype(F32)
        decay = jnp.exp(pick(totals, 2 * lax.div(z, 2) + 1))
        out_ref[i] = (decay * jnp.where(odd, got, keep) + jnp.where(odd, keep, got)).astype(BF16)
    count = keep_ref.shape[0]
    for j in range(out_ref.shape[0] - count):
        i = (1 - lax.div(z, 2)) * (count // 2) + j
        out_ref[count + j] = jnp.where(odd, got_ref[i], keep_ref[i])


def block_states(head_of, z_ref, pair_ref, got_ref, totals_ref, out_ref):
    z = z_ref[0]
    upper = z >= 2
    for i in range(out_ref.shape[0]):
        totals = totals_ref[head_of(i, z, 0)]
        mine, got = pair_ref[i].astype(F32), got_ref[i].astype(F32)
        decay = jnp.exp(pick(totals, 2) + pick(totals, 3))
        state = decay * jnp.where(upper, got, mine) + jnp.where(upper, mine, got)
        out_ref[i, :128, :] = state.astype(BF16)
        put_log(out_ref, (i,), jnp.sum(totals, axis=0, keepdims=True))


def scan_step(bit, s_ref, i, own_ref, got_ref, before, before_log):
    upper = (s_ref[1] >> bit) & 1 == 1
    own, got = own_ref[i, :128, :].astype(F32), got_ref[i, :128, :].astype(F32)
    own_log, got_log = get_log(own_ref, (i,)), get_log(got_ref, (i,))
    if before is None:
        after = jnp.where(upper, got, 0.0)
        after_log = jnp.where(upper, got_log, 0.0)
    else:
        after = jnp.where(upper, jnp.exp(before_log) * got + before, before)
        after_log = jnp.where(upper, before_log + got_log, before_log)
    total = jnp.exp(jnp.where(upper, own_log, got_log)) * jnp.where(upper, got, own) + jnp.where(upper, own, got)
    return after, after_log, total, own_log + got_log


def scan_blocks(bit, s_ref, own_ref, got_ref, *refs):
    before_ref = refs[0] if bit else None
    after_ref, total_ref = refs[-2:]
    for i in range(own_ref.shape[0]):
        before = before_ref[i, :128, :] if bit else None
        before_log = before_ref[i, 128:129, :] if bit else None
        after, after_log, total, total_log = scan_step(bit, s_ref, i, own_ref, got_ref, before, before_log)
        after_ref[i, :128, :] = after
        after_ref[i, 128:, :] = jnp.broadcast_to(after_log, (8, 128))
        total_ref[i, :128, :] = total.astype(BF16)
        put_log(total_ref, (i,), total_log)


def entering_states(first, heads, done, bit, s_ref, own_ref, got_ref, before_ref, keep_ref, keep_got_ref, pair_ref, pair_got_ref, totals_ref, *outs):
    z = s_ref[0]
    odd, upper = lax.rem(z, 2) == 1, z >= 2
    count = own_ref.shape[0]
    m = count // 2

    def parts_of(i, head):
        totals = totals_ref[head]
        state = scan_step(
            bit, s_ref, i, own_ref, got_ref, before_ref[i, :128, :], before_ref[i, 128:129, :]
        )[0]
        low = jnp.where(upper, pair_got_ref[i], pair_ref[i]).astype(F32)
        even_part = jnp.where(odd, keep_got_ref[i], keep_ref[i]).astype(F32)
        middle = jnp.exp(pick(totals, 0) + pick(totals, 1)) * state + low
        return totals, state, middle, even_part

    for i in range(count):
        n, j = divmod(i, m)
        if j < done:
            continue
        totals, state, middle, even_part = parts_of(i, (2 * n + lax.rem(z, 2)) * heads + first + j)
        even_state = jnp.where(upper, middle, state)
        odd_state = jnp.exp(pick(totals, jnp.where(upper, 2, 0))) * even_state + even_part
        at = n * (m - done) + j - done
        outs[0][at] = jnp.where(odd, odd_state, even_state).astype(BF16)
        outs[1][at] = jnp.where(odd, even_state, odd_state).astype(BF16)
    for j in range(done):
        totals, state, middle, even_part = parts_of(lax.div(z, 2) * m + j, z * heads + first + j)
        other = pair_got_ref[count + j].astype(F32)
        first_part, third_part = jnp.where(upper, other, even_part), jnp.where(upper, even_part, other)
        outs[2][j, 0] = state.astype(BF16)
        outs[2][j, 1] = (jnp.exp(pick(totals, 0)) * state + first_part).astype(BF16)
        outs[2][j, 2] = middle.astype(BF16)
        outs[2][j, 3] = (jnp.exp(pick(totals, 2)) * middle + third_part).astype(BF16)


def norm(mixture, gain):
    mean_square = jnp.mean(mixture * mixture, axis=1, keepdims=True)
    return (mixture * lax.rsqrt(mean_square + 1e-6) * gain).astype(BF16)


def column_of(row):
    return jnp.broadcast_to(row, (128, row.shape[1])).T


def mix_head(query, key, value, row, entering=None):
    rows = query.shape[0]
    chunk = min(CHUNK, rows)
    column = column_of(row)
    causal = lax.broadcasted_iota(jnp.int32, (chunk, chunk), 0) >= lax.broadcasted_iota(
        jnp.int32, (chunk, chunk), 1
    )
    state = None if entering is None else entering.astype(F32)
    start_level = jnp.zeros((1, 1), F32)
    pieces = []
    for start in range(0, rows, chunk):
        stop = start + chunk
        q, k, v = query[start:stop], key[start:stop], value[start:stop]
        r, c = row[:, start:stop], column[start:stop]
        scores = lax.dot_general(q, k, (((1,), (1,)), ((), ())), preferred_element_type=F32)
        gap = jnp.where(causal, jnp.concatenate([c] * (chunk // 128), axis=1) - r, -1e30)
        weights = (scores * jnp.exp(gap)).astype(BF16)
        mixture = jnp.dot(weights, v, preferred_element_type=F32)
        if state is not None:
            scaled = (q.astype(F32) * jnp.exp(c - start_level)).astype(BF16)
            mixture = mixture + jnp.dot(scaled, state.astype(BF16), preferred_element_type=F32)
        pieces.append(mixture)
        if stop < rows:
            end = row[:, stop - 1 : stop]
            added = state_of(k, v, r, end)
            state = added if state is None else jnp.exp(end - start_level) * state + added
            start_level = end
    return pieces


def attend(first, heads, states_of, s_ref, levels_ref, gains_ref, *refs):
    z = s_ref[0]
    parts = 4
    streams, outs = refs[-3 - parts : -parts], refs[-parts:]
    states = refs[: -3 - parts]
    rows = levels_ref.shape[1]

    def step(*blocks):
        j = pl.program_id(0)
        for k in range(parts):
            home = lax.rem(z + k, parts)
            at = pl.ds(home * heads + first + j, 1)
            query, key, value = blocks[3 * k : 3 * k + 3]
            pieces = mix_head(query[...], key[...], value[...], levels_ref[at, :], states_of(states, k, home, j))
            size = pieces[0].shape[0]
            for n, piece in enumerate(pieces):
                blocks[3 * parts + k][n * size : (n + 1) * size, :] = norm(piece, gains_ref[at, :])

    specs = [
        pl.BlockSpec((rows, 128), lambda j, k=k: (0, lax.rem(z + k, parts) * heads + first + j)) for k in range(parts)
    ]
    pltpu.emit_pipeline(
        step,
        grid=(outs[0].shape[1] // 128,),
        in_specs=[spec for spec in specs for _ in range(3)],
        out_specs=[pl.BlockSpec((rows, 128), lambda j: (0, j))] * parts,
    )(*list(streams) * parts, *outs)


def own_parts(first, heads, s_ref, levels_ref, queries_ref, keys_ref, values_ref, *outs):
    z = s_ref[0]
    parts = len(outs)
    rows = levels_ref.shape[1]
    count = outs[0].shape[1] // 256

    def step(*blocks):
        j = pl.program_id(0)
        for k in range(parts):
            head = lax.rem(z + k, parts) * heads + first + j
            query, key, value = blocks[3 * k : 3 * k + 3]
            pieces = mix_head(query[...], key[...], value[...], levels_ref[pl.ds(head, 1), :])
            size = pieces[0].shape[0]
            for n, piece in enumerate(pieces):
                outs[k][n * size : (n + 1) * size, pl.ds(pl.multiple_of(j * 128, 128), 128)] = piece.astype(BF16)
            outs[k][:, pl.ds(pl.multiple_of((count + j) * 128, 128), 128)] = query[...]

    specs = [
        pl.BlockSpec((rows, 128), lambda j, k=k: (0, lax.rem(z + k, parts) * heads + first + j)) for k in range(parts)
    ]
    pltpu.emit_pipeline(step, grid=(count,), in_specs=[spec for spec in specs for _ in range(3)])(
        *[queries_ref, keys_ref, values_ref] * parts
    )


def finish(first, heads, s_ref, decay_ref, gains_ref, states_ref, *refs):
    parts = len(refs) // 2
    z = s_ref[0]
    rows, width = refs[parts].shape
    upper = lax.broadcasted_iota(jnp.int32, (rows, rows), 0) <= lax.broadcasted_iota(jnp.int32, (rows, rows), 1)
    upper = jnp.where(upper, 1.0, 0.0).astype(F32)
    for k in range(parts):
        c = lax.rem(z + parts - k, parts)
        levels = jnp.dot(
            decay_ref[:, pl.ds(pl.multiple_of(c * rows, 128), rows)], upper,
            precision=lax.Precision.HIGHEST, preferred_element_type=F32,
        )
        for j in range(width // 128):
            column = column_of(levels[first + j : first + j + 1, :])
            at = slice(j * 128, (j + 1) * 128)
            query = refs[k][:, width + j * 128 : width + (j + 1) * 128]
            scaled = (query.astype(F32) * jnp.exp(column)).astype(BF16)
            mixture = refs[k][:, at].astype(F32) + jnp.dot(scaled, states_ref[j, c], preferred_element_type=F32)
            refs[parts + k][:, at] = norm(mixture, gains_ref[pl.ds(z * heads + first + j, 1), :])


def place(first, parts, s_ref, *refs):
    pieces, out_ref, sems = refs[:parts], refs[-2], refs[-1]
    rows, width = pieces[0].shape
    copies = []
    for k in range(parts):
        source = lax.rem(s_ref[0] + parts - k, parts)
        copies.append(
            pltpu.make_async_copy(
                pieces[k],
                out_ref.at[pl.ds(pl.multiple_of(source * rows, rows), rows), pl.ds(first * 128, width)],
                sems.at[k],
            )
        )
    for copy in copies:
        copy.start()
    for copy in copies:
        copy.wait()


def local(queries, keys, values, log_decay, gain):
    heads, block = log_decay.shape
    parts, blocks = lax.axis_size("grp"), lax.axis_size("seq")
    rows = queries.shape[0]
    call = Calls(jnp.stack([lax.axis_index("grp"), lax.axis_index("seq")]).astype(jnp.int32))

    def shift(x, k):
        return lax.ppermute(x, "grp", [(i, (i + k) % parts) for i in range(parts)])

    def swap(x, axis, bit):
        return lax.ppermute(x, axis, [(i, i ^ bit) for i in range(lax.axis_size(axis))])

    starts = [sum(group[0] for group in GROUPS[:g]) for g in range(len(GROUPS))]
    packed = call(
        pack_decays, [log_decay, gain.reshape(heads, 128)], [shape(heads, rows + 256, dtype=F32)] * parts,
        cost=cost_us(8),
    )
    got = [packed[0]] + [shift(packed[k], k) for k in range(1, parts)]
    levels, totals, gains = call(
        unpack_decays, got,
        [shape(heads * parts, rows, dtype=F32), shape(heads * parts, 8, 128, dtype=F32), shape(heads * parts, 128, dtype=F32)],
        scratch=[pltpu.VMEM((heads * parts, rows), F32)],
        cost=cost_us(8),
    )

    def outputs(first, m, states, states_of):
        outs = call(
            functools.partial(attend, first, heads, states_of), [levels, gains, *states],
            [shape(rows, m * 128)] * parts,
            streams=[queries, keys, values],
            cost=cost_us(2.5 * m),
        )
        return first, [outs[0]] + [shift(outs[k], k) for k in range(1, parts)]

    def travel(first, m, done, calls, home_states):
        n = 2 * m

        def head_of(i, z, other):
            return (2 * (i // m) + lax.rem(z + other, 2)) * heads + first + i % m

        keep, send = call(
            functools.partial(half_states, first, heads), [levels],
            [shape(n, 128, 128)] * 2,
            streams=[keys, values],
            cost=cost_us(m),
        )
        got = swap(send, "grp", 1)
        yield
        pair, = call(functools.partial(pair_states, head_of), [keep, got, totals], [shape(n + done, 128, 128)])
        pair_got = swap(pair, "grp", 2)
        yield
        total, = call(functools.partial(block_states, head_of), [pair, pair_got, totals], [shape(n, 144, 128)])
        before = []
        bits = blocks.bit_length() - 1
        for bit in range(bits - 1):
            other = swap(total, "seq", 1 << bit)
            yield
            after, total = call(
                functools.partial(scan_blocks, bit), [total, other, *before],
                [shape(n, 136, 128, dtype=F32), shape(n, 144, 128)],
            )
            before = [after]
        other = swap(total, "seq", 1 << (bits - 1))
        yield
        rest = m - done
        own, send, *home = call(
            functools.partial(entering_states, first, heads, done, bits - 1),
            [total, other, *before, keep, got, pair, pair_got, totals],
            [shape(2 * rest, 128, 128)] * 2 + [shape(done, parts, 128, 128)] * (done > 0),
        )
        home_states.extend(home)
        states = [own, swap(send, "grp", 1)]
        yield
        start = 0
        for count in calls:

            def states_of(refs, k, home, j, start=start):
                return refs[k % 2][lax.div(home, 2) * rest + start + j]

            yield outputs(first + done + start, count, states, states_of)
            start += count

    def finished(first, done, arrived, home_states):
        parcels = call(
            functools.partial(own_parts, first, heads), [levels], [shape(rows, 2 * done * 128)] * parts,
            streams=[queries, keys, values],
            cost=cost_us(2 * done),
        )
        arrived += [parcels[0]] + [shift(parcels[k], k) for k in range(1, parts)]
        yield
        yield first, call(
            functools.partial(finish, first, heads), [log_decay, gains, *home_states, *arrived],
            [shape(rows, done * 128)] * parts,
        )

    home_states = [[] for _ in GROUPS]
    work = [travel(first, *group, home) for first, group, home in zip(starts, GROUPS, home_states)]
    arrived = [[] for _ in GROUPS]
    home_work = [
        finished(first, group[1], parcels, home)
        for first, group, parcels, home in zip(starts, GROUPS, arrived, home_states)
    ]
    pieces, out = [[] for _ in GROUPS], None
    for action, g, *rest in ORDER:
        g = int(g)
        if action in "kh":
            piece = next(work[g] if action == "k" else home_work[g])
            if piece is not None:
                pieces[g].append(piece)
        elif action == "d":
            call.after.append(arrived[g][int(rest[0])])
        elif action == "w":
            call.after.append(pieces[g][int(rest[0])][1][int(rest[1])])
        else:
            first, piece = pieces[g][int(rest[0])]
            out, = call(
                functools.partial(place, first, parts), [*piece, *([] if out is None else [out])],
                [shape(block, heads * 128)],
                out_specs=[anywhere()],
                scratch=[pltpu.SemaphoreType.DMA((parts,))],
                aliases={} if out is None else {parts: 0},
            )
    return out


def solution(mesh):
    parts, blocks = mesh.shape["grp"], mesh.shape["seq"]
    fits = parts == 4 and blocks >= 4 and blocks & (blocks - 1) == 0
    in_specs = (
        P(("seq", "grp"), None),
        P(("seq", "grp"), None),
        P(("seq", "grp"), None),
        P("grp", "seq"),
        P("grp"),
    )
    out_specs = P("seq", "grp")
    return jax.shard_map(
        local if fits else local_any, mesh=mesh, in_specs=in_specs, out_specs=out_specs, check_vma=False
    )
```

```python
import functools

import jax
import jax.numpy as jnp
from jax import lax
from jax.experimental import pallas as pl
from jax.experimental.pallas import tpu as pltpu
from jax.sharding import PartitionSpec as P

GROUPS = ((3, 0, (1, 2)), (5, 0, (1, 2, 2)))
ORDER = ('k0', 'k1', 'k0', 'k0', 'k1', 'k0', 'k0', 'k1', 'k0', 'k1', 'k0', 'k1', 'w001', 'k0', 'w002', 'w003', 'k1', 'w011', 'k1', 'w012', 'w013', 'k1', 'w101', 'w103', 'k1', 'p00', 'p01', 'p10', 'p11', 'p12')
CHUNK = 256
VMEM_BYTES = 16 * 1024 * 1024
SCALE = 1.0e9
STREAM_VMEM_BYTES = 16 * 1024 * 1024
F32 = jnp.float32
BF16 = jnp.bfloat16


def entering_2(array, axis, combine, identity):
    length, mine = (lax.axis_size(axis), lax.axis_index(axis))
    everything = jax.tree.map(lambda part: lax.all_gather(part, axis), array)
    start = jax.tree.map(
        lambda part, zero: jnp.broadcast_to(jnp.asarray(zero, part.dtype), part.shape),
        array,
        identity,
    )

    def step(k, before):
        reached = k < mine
        new = combine(before, jax.tree.map(lambda part: part[k], everything))
        return jax.tree.map(lambda a, b: jnp.where(reached, a, b), new, before)

    return lax.fori_loop(0, length, step, start)


def local_mix(query_heads, key_heads, value_heads, levels):
    row_total = query_heads.shape[0]
    block_rows = min(512, row_total)
    pieces = []
    for start in range(0, row_total, block_rows):
        finish = start + block_rows
        scores = jnp.einsum(
            "thd,shd->hts",
            query_heads[start:finish],
            key_heads[:finish],
            preferred_element_type=jnp.float32,
        )
        causal = (
            jnp.arange(start, finish, dtype=jnp.int32)[:, None]
            >= jnp.arange(finish, dtype=jnp.int32)[None, :]
        )
        decay_gap = jnp.where(
            causal[None], levels[:, start:finish, None] - levels[:, None, :finish], 0.0
        )
        weights = jnp.where(causal[None], scores * jnp.exp(decay_gap), 0.0).astype(jnp.bfloat16)
        pieces.append(
            jnp.einsum(
                "hts,shd->thd", weights, value_heads[:finish], preferred_element_type=jnp.float32
            )
        )
    return jnp.concatenate(pieces, axis=0)


def local_any(queries, keys, values, log_decay, gain):
    head_count = log_decay.shape[0]
    row_count = log_decay.shape[1]
    head_width = gain.shape[0] // head_count
    query_rows, key_rows, value_rows = (
        lax.all_to_all(queries, "grp", split_axis=1, concat_axis=0, tiled=True),
        lax.all_to_all(keys, "grp", split_axis=1, concat_axis=0, tiled=True),
        lax.all_to_all(values, "grp", split_axis=1, concat_axis=0, tiled=True),
    )
    key_heads = key_rows.reshape(row_count, head_count, head_width)
    value_heads = value_rows.reshape(row_count, head_count, head_width)
    levels = jnp.cumsum(log_decay, axis=1)
    block_total = levels[:, -1]
    tail_decay = jnp.exp(block_total[:, None] - levels)
    scaled_keys = (key_heads.astype(jnp.float32) * tail_decay.T[:, :, None]).astype(jnp.bfloat16)
    block_state = jnp.einsum(
        "thd,the->hde", scaled_keys, value_heads, preferred_element_type=jnp.float32
    )

    def combine_blocks(earlier, later_part):
        return (
            earlier[0] + later_part[0],
            jnp.exp(later_part[0])[:, None, None] * earlier[1] + later_part[1],
        )

    identity = (jnp.zeros_like(block_total), jnp.zeros_like(block_state))
    _, entering = entering_2((block_total, block_state), "seq", combine_blocks, identity)
    query_heads = query_rows.reshape(row_count, head_count, head_width)
    local_part = local_mix(query_heads, key_heads, value_heads, levels)
    state_half = entering.astype(jnp.bfloat16)
    scaled_queries = (query_heads.astype(jnp.float32) * jnp.exp(levels).T[:, :, None]).astype(
        jnp.bfloat16
    )
    carried_part = jnp.einsum(
        "thd,hde->the", scaled_queries, state_half, preferred_element_type=jnp.float32
    )
    mixture = local_part + carried_part
    mean_square = jnp.mean(mixture * mixture, axis=2, keepdims=True)
    normed = mixture * lax.rsqrt(mean_square + 1e-06) * gain.reshape(head_count, head_width)[None]
    return normed.reshape(row_count, head_count * head_width).astype(jnp.bfloat16)


def in_vmem():
    return pl.BlockSpec(memory_space=pltpu.VMEM)


def anywhere():
    return pl.BlockSpec(memory_space=pl.ANY)


class Calls:
    def __init__(self, scalars):
        self.scalars, self.after = scalars, []

    def __call__(self, kernel, arrays, outs, streams=(), out_specs=None, scratch=(), cost=1000, aliases=None):
        count = len(arrays) + len(streams)
        after, self.after = [a for a in self.after if not any(a is b for b in arrays)], []

        def body(s_ref, *refs):
            kernel(s_ref, *refs[:count], *refs[count + len(after) :])

        results = pl.pallas_call(
            body,
            out_shape=outs,
            in_specs=[
                pl.BlockSpec(memory_space=pltpu.SMEM),
                *[anywhere() if aliases and n in aliases else in_vmem() for n in range(len(arrays))],
                *[pl.BlockSpec(memory_space=pltpu.HBM)] * len(streams),
                *[anywhere()] * len(after),
            ],
            out_specs=out_specs or [in_vmem()] * len(outs),
            scratch_shapes=list(scratch),
            compiler_params=pltpu.CompilerParams(vmem_limit_bytes=STREAM_VMEM_BYTES if streams else VMEM_BYTES),
            cost_estimate=pl.CostEstimate(flops=cost, bytes_accessed=1000, transcendentals=0),
            input_output_aliases={n + 1: o for n, o in (aliases or {}).items()},
        )(self.scalars, *arrays, *streams, *after)
        self.after.append(results[0])
        return results


def cost_us(time):
    return int(time * SCALE)


def shape(*dims, dtype=BF16):
    return jax.ShapeDtypeStruct(dims, dtype)


def pick(rows, index):
    at = lax.broadcasted_iota(jnp.int32, rows.shape, 0)
    return jnp.sum(jnp.where(at == index, rows, 0.0), axis=0, keepdims=True)


def pack_decays(s_ref, decay_ref, gain_ref, *out_refs):
    z = s_ref[0]
    heads, rows = decay_ref.shape
    parts = len(out_refs)
    width = rows // parts
    lane = lax.broadcasted_iota(jnp.int32, (heads, 128), 1)
    totals = jnp.zeros((heads, 128), F32)
    for c in range(parts):
        total = jnp.sum(decay_ref[:, c * width : (c + 1) * width], axis=1, keepdims=True)
        totals = jnp.where(lane == c, total, totals)
    for k, out_ref in enumerate(out_refs):
        to = lax.rem(z + k, parts)
        out_ref[:, :width] = decay_ref[:, pl.ds(pl.multiple_of(to * width, 128), width)]
        out_ref[:, width : width + 128] = totals
        out_ref[:, width + 128 :] = gain_ref[...]


def unpack_decays(z_ref, *refs):
    parts = len(refs) - 4
    ins, (levels_ref, totals_ref, gains_ref, decays) = refs[:parts], refs[parts:]
    z = z_ref[0]
    heads = ins[0].shape[0]
    width = decays.shape[1]
    for k, in_ref in enumerate(ins):
        home = lax.rem(z + parts - k, parts)
        at = pl.ds(pl.multiple_of(home * heads, heads), heads)
        decays[at, :] = in_ref[:, :width]
        gains_ref[at, :] = in_ref[:, width + 128 :]
        totals = in_ref[:, width : width + 128]
        row = lax.broadcasted_iota(jnp.int32, totals_ref.shape[1:], 0)
        for h in range(heads):
            rows = jnp.zeros(totals_ref.shape[1:], F32)
            for c in range(parts):
                rows = jnp.where(row == c, totals[h : h + 1, c : c + 1], rows)
            totals_ref[home * heads + h] = rows
    upper = lax.broadcasted_iota(jnp.int32, (width, width), 0) <= lax.broadcasted_iota(
        jnp.int32, (width, width), 1
    )
    levels_ref[...] = jnp.dot(
        decays[...],
        jnp.where(upper, 1.0, 0.0).astype(F32),
        precision=lax.Precision.HIGHEST,
        preferred_element_type=F32,
    )


def put_log(ref, i, log):
    high = log.astype(BF16).astype(F32)
    middle = (log - high).astype(BF16).astype(F32)
    low = log - high - middle
    row = lax.broadcasted_iota(jnp.int32, (16, 128), 0)
    rows = jnp.where(row == 0, high, jnp.where(row == 1, middle, jnp.where(row == 2, low, 0.0)))
    ref[(*i, pl.ds(ref.shape[-2] - 16, 16))] = rows.astype(BF16)


def get_log(ref, i):
    return jnp.sum(ref[(*i, pl.ds(ref.shape[-2] - 16, 16))].astype(F32), axis=0, keepdims=True)


def state_of(key, value, row, end):
    scaled = (key.T.astype(F32) * jnp.exp(end - row)).astype(BF16)
    return jnp.dot(scaled, value, preferred_element_type=F32)


def half_states(first, heads, s_ref, levels_ref, keys_ref, values_ref, keep_ref, send_ref):
    z = s_ref[0]
    m = keep_ref.shape[0] // 2
    rows = levels_ref.shape[1]
    places = [(out, n, 2 * n + lax.rem(z + other, 2)) for other, out in enumerate((keep_ref, send_ref)) for n in range(2)]

    def step(*refs):
        j = pl.program_id(0)
        for k, (out, n, home) in enumerate(places):
            row = levels_ref[pl.ds(home * heads + first + j, 1), :]
            state = state_of(refs[2 * k][...], refs[2 * k + 1][...], row, row[:, rows - 1 :])
            out[n * m + j] = state.astype(BF16)

    specs = [pl.BlockSpec((rows, 128), lambda j, home=home: (0, home * heads + first + j)) for _, _, home in places]
    pltpu.emit_pipeline(step, grid=(m,), in_specs=[spec for spec in specs for _ in range(2)])(
        *[keys_ref, values_ref] * len(places)
    )


def pair_states(head_of, z_ref, keep_ref, got_ref, totals_ref, out_ref):
    z = z_ref[0]
    odd = lax.rem(z, 2) == 1
    for i in range(keep_ref.shape[0]):
        totals = totals_ref[head_of(i, z, 0)]
        keep, got = keep_ref[i].astype(F32), got_ref[i].astype(F32)
        decay = jnp.exp(pick(totals, 2 * lax.div(z, 2) + 1))
        out_ref[i] = (decay * jnp.where(odd, got, keep) + jnp.where(odd, keep, got)).astype(BF16)
    count = keep_ref.shape[0]
    for j in range(out_ref.shape[0] - count):
        i = (1 - lax.div(z, 2)) * (count // 2) + j
        out_ref[count + j] = jnp.where(odd, got_ref[i], keep_ref[i])


def block_states(head_of, z_ref, pair_ref, got_ref, totals_ref, out_ref):
    z = z_ref[0]
    upper = z >= 2
    for i in range(out_ref.shape[0]):
        totals = totals_ref[head_of(i, z, 0)]
        mine, got = pair_ref[i].astype(F32), got_ref[i].astype(F32)
        decay = jnp.exp(pick(totals, 2) + pick(totals, 3))
        state = decay * jnp.where(upper, got, mine) + jnp.where(upper, mine, got)
        out_ref[i, :128, :] = state.astype(BF16)
        put_log(out_ref, (i,), jnp.sum(totals, axis=0, keepdims=True))


def scan_step(bit, s_ref, i, own_ref, got_ref, before, before_log):
    upper = (s_ref[1] >> bit) & 1 == 1
    own, got = own_ref[i, :128, :].astype(F32), got_ref[i, :128, :].astype(F32)
    own_log, got_log = get_log(own_ref, (i,)), get_log(got_ref, (i,))
    if before is None:
        after = jnp.where(upper, got, 0.0)
        after_log = jnp.where(upper, got_log, 0.0)
    else:
        after = jnp.where(upper, jnp.exp(before_log) * got + before, before)
        after_log = jnp.where(upper, before_log + got_log, before_log)
    total = jnp.exp(jnp.where(upper, own_log, got_log)) * jnp.where(upper, got, own) + jnp.where(upper, own, got)
    return after, after_log, total, own_log + got_log


def scan_blocks(bit, s_ref, own_ref, got_ref, *refs):
    before_ref = refs[0] if bit else None
    after_ref, total_ref = refs[-2:]
    for i in range(own_ref.shape[0]):
        before = before_ref[i, :128, :] if bit else None
        before_log = before_ref[i, 128:129, :] if bit else None
        after, after_log, total, total_log = scan_step(bit, s_ref, i, own_ref, got_ref, before, before_log)
        after_ref[i, :128, :] = after
        after_ref[i, 128:, :] = jnp.broadcast_to(after_log, (8, 128))
        total_ref[i, :128, :] = total.astype(BF16)
        put_log(total_ref, (i,), total_log)


def entering_states(first, heads, done, bit, s_ref, own_ref, got_ref, before_ref, keep_ref, keep_got_ref, pair_ref, pair_got_ref, totals_ref, *outs):
    z = s_ref[0]
    odd, upper = lax.rem(z, 2) == 1, z >= 2
    count = own_ref.shape[0]
    m = count // 2

    def parts_of(i, head):
        totals = totals_ref[head]
        state = scan_step(
            bit, s_ref, i, own_ref, got_ref, before_ref[i, :128, :], before_ref[i, 128:129, :]
        )[0]
        low = jnp.where(upper, pair_got_ref[i], pair_ref[i]).astype(F32)
        even_part = jnp.where(odd, keep_got_ref[i], keep_ref[i]).astype(F32)
        middle = jnp.exp(pick(totals, 0) + pick(totals, 1)) * state + low
        return totals, state, middle, even_part

    for i in range(count):
        n, j = divmod(i, m)
        if j < done:
            continue
        totals, state, middle, even_part = parts_of(i, (2 * n + lax.rem(z, 2)) * heads + first + j)
        even_state = jnp.where(upper, middle, state)
        odd_state = jnp.exp(pick(totals, jnp.where(upper, 2, 0))) * even_state + even_part
        at = n * (m - done) + j - done
        outs[0][at] = jnp.where(odd, odd_state, even_state).astype(BF16)
        outs[1][at] = jnp.where(odd, even_state, odd_state).astype(BF16)
    for j in range(done):
        totals, state, middle, even_part = parts_of(lax.div(z, 2) * m + j, z * heads + first + j)
        other = pair_got_ref[count + j].astype(F32)
        first_part, third_part = jnp.where(upper, other, even_part), jnp.where(upper, even_part, other)
        outs[2][j, 0] = state.astype(BF16)
        outs[2][j, 1] = (jnp.exp(pick(totals, 0)) * state + first_part).astype(BF16)
        outs[2][j, 2] = middle.astype(BF16)
        outs[2][j, 3] = (jnp.exp(pick(totals, 2)) * middle + third_part).astype(BF16)


def norm(mixture, gain):
    mean_square = jnp.mean(mixture * mixture, axis=1, keepdims=True)
    return (mixture * lax.rsqrt(mean_square + 1e-6) * gain).astype(BF16)


def column_of(row):
    return jnp.broadcast_to(row, (128, row.shape[1])).T


def mix_head(query, key, value, row, entering=None):
    rows = query.shape[0]
    chunk = min(CHUNK, rows)
    column = column_of(row)
    causal = lax.broadcasted_iota(jnp.int32, (chunk, chunk), 0) >= lax.broadcasted_iota(
        jnp.int32, (chunk, chunk), 1
    )
    state = None if entering is None else entering.astype(F32)
    start_level = jnp.zeros((1, 1), F32)
    pieces = []
    for start in range(0, rows, chunk):
        stop = start + chunk
        q, k, v = query[start:stop], key[start:stop], value[start:stop]
        r, c = row[:, start:stop], column[start:stop]
        scores = lax.dot_general(q, k, (((1,), (1,)), ((), ())), preferred_element_type=F32)
        gap = jnp.where(causal, jnp.concatenate([c] * (chunk // 128), axis=1) - r, -1e30)
        weights = (scores * jnp.exp(gap)).astype(BF16)
        mixture = jnp.dot(weights, v, preferred_element_type=F32)
        if state is not None:
            scaled = (q.astype(F32) * jnp.exp(c - start_level)).astype(BF16)
            mixture = mixture + jnp.dot(scaled, state.astype(BF16), preferred_element_type=F32)
        pieces.append(mixture)
        if stop < rows:
            end = row[:, stop - 1 : stop]
            added = state_of(k, v, r, end)
            state = added if state is None else jnp.exp(end - start_level) * state + added
            start_level = end
    return pieces


def attend(first, heads, states_of, s_ref, levels_ref, gains_ref, *refs):
    z = s_ref[0]
    parts = 4
    streams, outs = refs[-3 - parts : -parts], refs[-parts:]
    states = refs[: -3 - parts]
    rows = levels_ref.shape[1]

    def step(*blocks):
        j = pl.program_id(0)
        for k in range(parts):
            home = lax.rem(z + k, parts)
            at = pl.ds(home * heads + first + j, 1)
            query, key, value = blocks[3 * k : 3 * k + 3]
            pieces = mix_head(query[...], key[...], value[...], levels_ref[at, :], states_of(states, k, home, j))
            size = pieces[0].shape[0]
            for n, piece in enumerate(pieces):
                blocks[3 * parts + k][n * size : (n + 1) * size, :] = norm(piece, gains_ref[at, :])

    specs = [
        pl.BlockSpec((rows, 128), lambda j, k=k: (0, lax.rem(z + k, parts) * heads + first + j)) for k in range(parts)
    ]
    pltpu.emit_pipeline(
        step,
        grid=(outs[0].shape[1] // 128,),
        in_specs=[spec for spec in specs for _ in range(3)],
        out_specs=[pl.BlockSpec((rows, 128), lambda j: (0, j))] * parts,
    )(*list(streams) * parts, *outs)


def own_parts(first, heads, s_ref, levels_ref, queries_ref, keys_ref, values_ref, *outs):
    z = s_ref[0]
    parts = len(outs)
    rows = levels_ref.shape[1]
    count = outs[0].shape[1] // 256

    def step(*blocks):
        j = pl.program_id(0)
        for k in range(parts):
            head = lax.rem(z + k, parts) * heads + first + j
            query, key, value = blocks[3 * k : 3 * k + 3]
            pieces = mix_head(query[...], key[...], value[...], levels_ref[pl.ds(head, 1), :])
            size = pieces[0].shape[0]
            for n, piece in enumerate(pieces):
                outs[k][n * size : (n + 1) * size, pl.ds(pl.multiple_of(j * 128, 128), 128)] = piece.astype(BF16)
            outs[k][:, pl.ds(pl.multiple_of((count + j) * 128, 128), 128)] = query[...]

    specs = [
        pl.BlockSpec((rows, 128), lambda j, k=k: (0, lax.rem(z + k, parts) * heads + first + j)) for k in range(parts)
    ]
    pltpu.emit_pipeline(step, grid=(count,), in_specs=[spec for spec in specs for _ in range(3)])(
        *[queries_ref, keys_ref, values_ref] * parts
    )


def finish(first, heads, s_ref, decay_ref, gains_ref, states_ref, *refs):
    parts = len(refs) // 2
    z = s_ref[0]
    rows, width = refs[parts].shape
    upper = lax.broadcasted_iota(jnp.int32, (rows, rows), 0) <= lax.broadcasted_iota(jnp.int32, (rows, rows), 1)
    upper = jnp.where(upper, 1.0, 0.0).astype(F32)
    for k in range(parts):
        c = lax.rem(z + parts - k, parts)
        levels = jnp.dot(
            decay_ref[:, pl.ds(pl.multiple_of(c * rows, 128), rows)], upper,
            precision=lax.Precision.HIGHEST, preferred_element_type=F32,
        )
        for j in range(width // 128):
            column = column_of(levels[first + j : first + j + 1, :])
            at = slice(j * 128, (j + 1) * 128)
            query = refs[k][:, width + j * 128 : width + (j + 1) * 128]
            scaled = (query.astype(F32) * jnp.exp(column)).astype(BF16)
            mixture = refs[k][:, at].astype(F32) + jnp.dot(scaled, states_ref[j, c], preferred_element_type=F32)
            refs[parts + k][:, at] = norm(mixture, gains_ref[pl.ds(z * heads + first + j, 1), :])


def place(first, parts, s_ref, *refs):
    pieces, out_ref, sems = refs[:parts], refs[-2], refs[-1]
    rows, width = pieces[0].shape
    copies = []
    for k in range(parts):
        source = lax.rem(s_ref[0] + parts - k, parts)
        copies.append(
            pltpu.make_async_copy(
                pieces[k],
                out_ref.at[pl.ds(pl.multiple_of(source * rows, rows), rows), pl.ds(first * 128, width)],
                sems.at[k],
            )
        )
    for copy in copies:
        copy.start()
    for copy in copies:
        copy.wait()


def local(queries, keys, values, log_decay, gain):
    heads, block = log_decay.shape
    parts, blocks = lax.axis_size("grp"), lax.axis_size("seq")
    rows = queries.shape[0]
    call = Calls(jnp.stack([lax.axis_index("grp"), lax.axis_index("seq")]).astype(jnp.int32))

    def shift(x, k):
        return lax.ppermute(x, "grp", [(i, (i + k) % parts) for i in range(parts)])

    def swap(x, axis, bit):
        return lax.ppermute(x, axis, [(i, i ^ bit) for i in range(lax.axis_size(axis))])

    starts = [sum(group[0] for group in GROUPS[:g]) for g in range(len(GROUPS))]
    packed = call(
        pack_decays, [log_decay, gain.reshape(heads, 128)], [shape(heads, rows + 256, dtype=F32)] * parts,
        cost=cost_us(8),
    )
    got = [packed[0]] + [shift(packed[k], k) for k in range(1, parts)]
    levels, totals, gains = call(
        unpack_decays, got,
        [shape(heads * parts, rows, dtype=F32), shape(heads * parts, 8, 128, dtype=F32), shape(heads * parts, 128, dtype=F32)],
        scratch=[pltpu.VMEM((heads * parts, rows), F32)],
    )

    def outputs(first, m, states, states_of):
        outs = call(
            functools.partial(attend, first, heads, states_of), [levels, gains, *states],
            [shape(rows, m * 128)] * parts,
            streams=[queries, keys, values],
            cost=cost_us(2.5 * m),
        )
        return first, [outs[0]] + [shift(outs[k], k) for k in range(1, parts)]

    def travel(first, m, done, calls, home_states):
        n = 2 * m

        def head_of(i, z, other):
            return (2 * (i // m) + lax.rem(z + other, 2)) * heads + first + i % m

        keep, send = call(
            functools.partial(half_states, first, heads), [levels],
            [shape(n, 128, 128)] * 2,
            streams=[keys, values],
            cost=cost_us(m),
        )
        got = swap(send, "grp", 1)
        yield
        pair, = call(functools.partial(pair_states, head_of), [keep, got, totals], [shape(n + done, 128, 128)])
        pair_got = swap(pair, "grp", 2)
        yield
        total, = call(functools.partial(block_states, head_of), [pair, pair_got, totals], [shape(n, 144, 128)])
        before = []
        bits = blocks.bit_length() - 1
        for bit in range(bits - 1):
            other = swap(total, "seq", 1 << bit)
            yield
            after, total = call(
                functools.partial(scan_blocks, bit), [total, other, *before],
                [shape(n, 136, 128, dtype=F32), shape(n, 144, 128)],
            )
            before = [after]
        other = swap(total, "seq", 1 << (bits - 1))
        yield
        rest = m - done
        own, send, *home = call(
            functools.partial(entering_states, first, heads, done, bits - 1),
            [total, other, *before, keep, got, pair, pair_got, totals],
            [shape(2 * rest, 128, 128)] * 2 + [shape(done, parts, 128, 128)] * (done > 0),
        )
        home_states.extend(home)
        states = [own, swap(send, "grp", 1)]
        yield
        start = 0
        for count in calls:

            def states_of(refs, k, home, j, start=start):
                return refs[k % 2][lax.div(home, 2) * rest + start + j]

            yield outputs(first + done + start, count, states, states_of)
            start += count

    def finished(first, done, arrived, home_states):
        parcels = call(
            functools.partial(own_parts, first, heads), [levels], [shape(rows, 2 * done * 128)] * parts,
            streams=[queries, keys, values],
            cost=cost_us(2 * done),
        )
        arrived += [parcels[0]] + [shift(parcels[k], k) for k in range(1, parts)]
        yield
        yield first, call(
            functools.partial(finish, first, heads), [log_decay, gains, *home_states, *arrived],
            [shape(rows, done * 128)] * parts,
        )

    home_states = [[] for _ in GROUPS]
    work = [travel(first, *group, home) for first, group, home in zip(starts, GROUPS, home_states)]
    arrived = [[] for _ in GROUPS]
    home_work = [
        finished(first, group[1], parcels, home)
        for first, group, parcels, home in zip(starts, GROUPS, arrived, home_states)
    ]
    pieces, out = [[] for _ in GROUPS], None
    for action, g, *rest in ORDER:
        g = int(g)
        if action in "kh":
            piece = next(work[g] if action == "k" else home_work[g])
            if piece is not None:
                pieces[g].append(piece)
        elif action == "d":
            call.after.append(arrived[g][int(rest[0])])
        elif action == "w":
            call.after.append(pieces[g][int(rest[0])][1][int(rest[1])])
        else:
            first, piece = pieces[g][int(rest[0])]
            out, = call(
                functools.partial(place, first, parts), [*piece, *([] if out is None else [out])],
                [shape(block, heads * 128)],
                out_specs=[anywhere()],
                scratch=[pltpu.SemaphoreType.DMA((parts,))],
                aliases={} if out is None else {parts: 0},
            )
    return out


def solution(mesh):
    parts, blocks = mesh.shape["grp"], mesh.shape["seq"]
    fits = parts == 4 and blocks >= 4 and blocks & (blocks - 1) == 0
    in_specs = (
        P(("seq", "grp"), None),
        P(("seq", "grp"), None),
        P(("seq", "grp"), None),
        P("grp", "seq"),
        P("grp"),
    )
    out_specs = P("seq", "grp")
    return jax.shard_map(
        local if fits else local_any, mesh=mesh, in_specs=in_specs, out_specs=out_specs, check_vma=False
    )
```

```python
import functools

import jax
import jax.numpy as jnp
from jax import lax
from jax.experimental import pallas as pl
from jax.experimental.pallas import tpu as pltpu
from jax.sharding import PartitionSpec as P

GROUPS = ((3, 0, (1, 2)), (5, 0, (1, 2, 2)))
ORDER = ('k0', 'k1', 'k0', 'k0', 'k1', 'k0', 'k0', 'k1', 'k0', 'k1', 'k0', 'k1', 'w001', 'k0', 'w002', 'w003', 'k1', 'w011', 'k1', 'w012', 'w013', 'k1', 'w101', 'w103', 'k1', 'p00', 'p01', 'p10', 'p11', 'p12')
CHUNK = 256
VMEM_BYTES = 16 * 1024 * 1024
SCALE = 1.0e9
STREAM_VMEM_BYTES = 16 * 1024 * 1024
F32 = jnp.float32
BF16 = jnp.bfloat16


def entering_2(array, axis, combine, identity):
    length, mine = (lax.axis_size(axis), lax.axis_index(axis))
    everything = jax.tree.map(lambda part: lax.all_gather(part, axis), array)
    start = jax.tree.map(
        lambda part, zero: jnp.broadcast_to(jnp.asarray(zero, part.dtype), part.shape),
        array,
        identity,
    )

    def step(k, before):
        reached = k < mine
        new = combine(before, jax.tree.map(lambda part: part[k], everything))
        return jax.tree.map(lambda a, b: jnp.where(reached, a, b), new, before)

    return lax.fori_loop(0, length, step, start)


def local_mix(query_heads, key_heads, value_heads, levels):
    row_total = query_heads.shape[0]
    block_rows = min(512, row_total)
    pieces = []
    for start in range(0, row_total, block_rows):
        finish = start + block_rows
        scores = jnp.einsum(
            "thd,shd->hts",
            query_heads[start:finish],
            key_heads[:finish],
            preferred_element_type=jnp.float32,
        )
        causal = (
            jnp.arange(start, finish, dtype=jnp.int32)[:, None]
            >= jnp.arange(finish, dtype=jnp.int32)[None, :]
        )
        decay_gap = jnp.where(
            causal[None], levels[:, start:finish, None] - levels[:, None, :finish], 0.0
        )
        weights = jnp.where(causal[None], scores * jnp.exp(decay_gap), 0.0).astype(jnp.bfloat16)
        pieces.append(
            jnp.einsum(
                "hts,shd->thd", weights, value_heads[:finish], preferred_element_type=jnp.float32
            )
        )
    return jnp.concatenate(pieces, axis=0)


def local_any(queries, keys, values, log_decay, gain):
    head_count = log_decay.shape[0]
    row_count = log_decay.shape[1]
    head_width = gain.shape[0] // head_count
    query_rows, key_rows, value_rows = (
        lax.all_to_all(queries, "grp", split_axis=1, concat_axis=0, tiled=True),
        lax.all_to_all(keys, "grp", split_axis=1, concat_axis=0, tiled=True),
        lax.all_to_all(values, "grp", split_axis=1, concat_axis=0, tiled=True),
    )
    key_heads = key_rows.reshape(row_count, head_count, head_width)
    value_heads = value_rows.reshape(row_count, head_count, head_width)
    levels = jnp.cumsum(log_decay, axis=1)
    block_total = levels[:, -1]
    tail_decay = jnp.exp(block_total[:, None] - levels)
    scaled_keys = (key_heads.astype(jnp.float32) * tail_decay.T[:, :, None]).astype(jnp.bfloat16)
    block_state = jnp.einsum(
        "thd,the->hde", scaled_keys, value_heads, preferred_element_type=jnp.float32
    )

    def combine_blocks(earlier, later_part):
        return (
            earlier[0] + later_part[0],
            jnp.exp(later_part[0])[:, None, None] * earlier[1] + later_part[1],
        )

    identity = (jnp.zeros_like(block_total), jnp.zeros_like(block_state))
    _, entering = entering_2((block_total, block_state), "seq", combine_blocks, identity)
    query_heads = query_rows.reshape(row_count, head_count, head_width)
    local_part = local_mix(query_heads, key_heads, value_heads, levels)
    state_half = entering.astype(jnp.bfloat16)
    scaled_queries = (query_heads.astype(jnp.float32) * jnp.exp(levels).T[:, :, None]).astype(
        jnp.bfloat16
    )
    carried_part = jnp.einsum(
        "thd,hde->the", scaled_queries, state_half, preferred_element_type=jnp.float32
    )
    mixture = local_part + carried_part
    mean_square = jnp.mean(mixture * mixture, axis=2, keepdims=True)
    normed = mixture * lax.rsqrt(mean_square + 1e-06) * gain.reshape(head_count, head_width)[None]
    return normed.reshape(row_count, head_count * head_width).astype(jnp.bfloat16)


def in_vmem():
    return pl.BlockSpec(memory_space=pltpu.VMEM)


def anywhere():
    return pl.BlockSpec(memory_space=pl.ANY)


class Calls:
    def __init__(self, scalars):
        self.scalars, self.after = scalars, []

    def __call__(self, kernel, arrays, outs, streams=(), out_specs=None, scratch=(), cost=1000, aliases=None):
        count = len(arrays) + len(streams)
        after, self.after = [a for a in self.after if not any(a is b for b in arrays)], []

        def body(s_ref, *refs):
            kernel(s_ref, *refs[:count], *refs[count + len(after) :])

        results = pl.pallas_call(
            body,
            out_shape=outs,
            in_specs=[
                pl.BlockSpec(memory_space=pltpu.SMEM),
                *[anywhere() if aliases and n in aliases else in_vmem() for n in range(len(arrays))],
                *[pl.BlockSpec(memory_space=pltpu.HBM)] * len(streams),
                *[anywhere()] * len(after),
            ],
            out_specs=out_specs or [in_vmem()] * len(outs),
            scratch_shapes=list(scratch),
            compiler_params=pltpu.CompilerParams(vmem_limit_bytes=STREAM_VMEM_BYTES if streams else VMEM_BYTES),
            cost_estimate=pl.CostEstimate(flops=cost, bytes_accessed=1000, transcendentals=0),
            input_output_aliases={n + 1: o for n, o in (aliases or {}).items()},
        )(self.scalars, *arrays, *streams, *after)
        self.after.append(results[0])
        return results


def cost_us(time):
    return int(time * SCALE)


def shape(*dims, dtype=BF16):
    return jax.ShapeDtypeStruct(dims, dtype)


def pick(rows, index):
    at = lax.broadcasted_iota(jnp.int32, rows.shape, 0)
    return jnp.sum(jnp.where(at == index, rows, 0.0), axis=0, keepdims=True)


def pack_decays(s_ref, decay_ref, gain_ref, *out_refs):
    z = s_ref[0]
    heads, rows = decay_ref.shape
    parts = len(out_refs)
    width = rows // parts
    lane = lax.broadcasted_iota(jnp.int32, (heads, 128), 1)
    totals = jnp.zeros((heads, 128), F32)
    for c in range(parts):
        total = jnp.sum(decay_ref[:, c * width : (c + 1) * width], axis=1, keepdims=True)
        totals = jnp.where(lane == c, total, totals)
    for k, out_ref in enumerate(out_refs):
        to = lax.rem(z + k, parts)
        out_ref[:, :width] = decay_ref[:, pl.ds(pl.multiple_of(to * width, 128), width)]
        out_ref[:, width : width + 128] = totals
        out_ref[:, width + 128 :] = gain_ref[...]


def unpack_decays(z_ref, *refs):
    parts = len(refs) - 4
    ins, (levels_ref, totals_ref, gains_ref, decays) = refs[:parts], refs[parts:]
    z = z_ref[0]
    heads = ins[0].shape[0]
    width = decays.shape[1]
    for k, in_ref in enumerate(ins):
        home = lax.rem(z + parts - k, parts)
        at = pl.ds(pl.multiple_of(home * heads, heads), heads)
        decays[at, :] = in_ref[:, :width]
        gains_ref[at, :] = in_ref[:, width + 128 :]
        totals = in_ref[:, width : width + 128]
        row = lax.broadcasted_iota(jnp.int32, totals_ref.shape[1:], 0)
        for h in range(heads):
            rows = jnp.zeros(totals_ref.shape[1:], F32)
            for c in range(parts):
                rows = jnp.where(row == c, totals[h : h + 1, c : c + 1], rows)
            totals_ref[home * heads + h] = rows
    upper = lax.broadcasted_iota(jnp.int32, (width, width), 0) <= lax.broadcasted_iota(
        jnp.int32, (width, width), 1
    )
    levels_ref[...] = jnp.dot(
        decays[...],
        jnp.where(upper, 1.0, 0.0).astype(F32),
        precision=lax.Precision.HIGHEST,
        preferred_element_type=F32,
    )


def add_log(rows, i, log):
    high = log.astype(BF16).astype(F32)
    middle = (log - high).astype(BF16).astype(F32)
    low = log - high - middle
    at = lax.broadcasted_iota(jnp.int32, rows.shape, 0)
    for n, part in enumerate((high, middle, low)):
        rows = jnp.where(at == 3 * i + n, part, rows)
    return rows


def log_rows(n):
    return -(-3 * n // 16) * 16


def get_log(ref, i, count):
    rows = ref[pl.ds(count * 128, ref.shape[0] - count * 128), :].astype(F32)
    at = lax.broadcasted_iota(jnp.int32, rows.shape, 0)
    mine = (at >= 3 * i) & (at < 3 * i + 3)
    return jnp.sum(jnp.where(mine, rows, 0.0), axis=0, keepdims=True)


def get_state(ref, i):
    return ref[pl.ds(i * 128, 128), :].astype(F32)


def state_of(key, value, row, end):
    scaled = (key.T.astype(F32) * jnp.exp(end - row)).astype(BF16)
    return jnp.dot(scaled, value, preferred_element_type=F32)


def half_states(first, heads, s_ref, levels_ref, keys_ref, values_ref, keep_ref, send_ref):
    z = s_ref[0]
    m = keep_ref.shape[0] // 2
    rows = levels_ref.shape[1]
    places = [(out, n, 2 * n + lax.rem(z + other, 2)) for other, out in enumerate((keep_ref, send_ref)) for n in range(2)]

    def step(*refs):
        j = pl.program_id(0)
        for k, (out, n, home) in enumerate(places):
            row = levels_ref[pl.ds(home * heads + first + j, 1), :]
            state = state_of(refs[2 * k][...], refs[2 * k + 1][...], row, row[:, rows - 1 :])
            out[n * m + j] = state.astype(BF16)

    specs = [pl.BlockSpec((rows, 128), lambda j, home=home: (0, home * heads + first + j)) for _, _, home in places]
    pltpu.emit_pipeline(step, grid=(m,), in_specs=[spec for spec in specs for _ in range(2)])(
        *[keys_ref, values_ref] * len(places)
    )


def pair_states(head_of, z_ref, keep_ref, got_ref, totals_ref, out_ref):
    z = z_ref[0]
    odd = lax.rem(z, 2) == 1
    for i in range(keep_ref.shape[0]):
        totals = totals_ref[head_of(i, z, 0)]
        keep, got = keep_ref[i].astype(F32), got_ref[i].astype(F32)
        decay = jnp.exp(pick(totals, 2 * lax.div(z, 2) + 1))
        out_ref[i] = (decay * jnp.where(odd, got, keep) + jnp.where(odd, keep, got)).astype(BF16)
    count = keep_ref.shape[0]
    for j in range(out_ref.shape[0] - count):
        i = (1 - lax.div(z, 2)) * (count // 2) + j
        out_ref[count + j] = jnp.where(odd, got_ref[i], keep_ref[i])


def block_states(head_of, z_ref, pair_ref, got_ref, totals_ref, out_ref):
    z = z_ref[0]
    upper = z >= 2
    count = out_ref.shape[0] // 128
    logs = jnp.zeros((log_rows(count), 128), F32)
    for i in range(count):
        totals = totals_ref[head_of(i, z, 0)]
        mine, got = pair_ref[i].astype(F32), got_ref[i].astype(F32)
        decay = jnp.exp(pick(totals, 2) + pick(totals, 3))
        state = decay * jnp.where(upper, got, mine) + jnp.where(upper, mine, got)
        out_ref[i * 128 : (i + 1) * 128, :] = state.astype(BF16)
        logs = add_log(logs, i, jnp.sum(totals, axis=0, keepdims=True))
    out_ref[count * 128 :, :] = logs.astype(BF16)


def scan_step(bit, s_ref, i, count, own_ref, got_ref, before, before_log):
    upper = (s_ref[1] >> bit) & 1 == 1
    own, got = get_state(own_ref, i), get_state(got_ref, i)
    own_log, got_log = get_log(own_ref, i, count), get_log(got_ref, i, count)
    if before is None:
        after = jnp.where(upper, got, 0.0)
        after_log = jnp.where(upper, got_log, 0.0)
    else:
        after = jnp.where(upper, jnp.exp(before_log) * got + before, before)
        after_log = jnp.where(upper, before_log + got_log, before_log)
    total = jnp.exp(jnp.where(upper, own_log, got_log)) * jnp.where(upper, got, own) + jnp.where(upper, own, got)
    return after, after_log, total, own_log + got_log


def scan_blocks(bit, s_ref, own_ref, got_ref, *refs):
    before_ref = refs[0] if bit else None
    after_ref, total_ref = refs[-2:]
    count = after_ref.shape[0]
    logs = jnp.zeros((log_rows(count), 128), F32)
    for i in range(count):
        before = before_ref[i, :128, :] if bit else None
        before_log = before_ref[i, 128:129, :] if bit else None
        after, after_log, total, total_log = scan_step(bit, s_ref, i, count, own_ref, got_ref, before, before_log)
        after_ref[i, :128, :] = after
        after_ref[i, 128:, :] = jnp.broadcast_to(after_log, (8, 128))
        total_ref[i * 128 : (i + 1) * 128, :] = total.astype(BF16)
        logs = add_log(logs, i, total_log)
    total_ref[count * 128 :, :] = logs.astype(BF16)


def entering_states(first, heads, done, bit, s_ref, own_ref, got_ref, before_ref, keep_ref, keep_got_ref, pair_ref, pair_got_ref, totals_ref, *outs):
    z = s_ref[0]
    odd, upper = lax.rem(z, 2) == 1, z >= 2
    count = before_ref.shape[0]
    m = count // 2

    def parts_of(i, head):
        totals = totals_ref[head]
        state = scan_step(
            bit, s_ref, i, count, own_ref, got_ref, before_ref[i, :128, :], before_ref[i, 128:129, :]
        )[0]
        low = jnp.where(upper, pair_got_ref[i], pair_ref[i]).astype(F32)
        even_part = jnp.where(odd, keep_got_ref[i], keep_ref[i]).astype(F32)
        middle = jnp.exp(pick(totals, 0) + pick(totals, 1)) * state + low
        return totals, state, middle, even_part

    for i in range(count):
        n, j = divmod(i, m)
        if j < done:
            continue
        totals, state, middle, even_part = parts_of(i, (2 * n + lax.rem(z, 2)) * heads + first + j)
        even_state = jnp.where(upper, middle, state)
        odd_state = jnp.exp(pick(totals, jnp.where(upper, 2, 0))) * even_state + even_part
        at = n * (m - done) + j - done
        outs[0][at] = jnp.where(odd, odd_state, even_state).astype(BF16)
        outs[1][at] = jnp.where(odd, even_state, odd_state).astype(BF16)
    for j in range(done):
        totals, state, middle, even_part = parts_of(lax.div(z, 2) * m + j, z * heads + first + j)
        other = pair_got_ref[count + j].astype(F32)
        first_part, third_part = jnp.where(upper, other, even_part), jnp.where(upper, even_part, other)
        outs[2][j, 0] = state.astype(BF16)
        outs[2][j, 1] = (jnp.exp(pick(totals, 0)) * state + first_part).astype(BF16)
        outs[2][j, 2] = middle.astype(BF16)
        outs[2][j, 3] = (jnp.exp(pick(totals, 2)) * middle + third_part).astype(BF16)


def norm(mixture, gain):
    mean_square = jnp.mean(mixture * mixture, axis=1, keepdims=True)
    return (mixture * lax.rsqrt(mean_square + 1e-6) * gain).astype(BF16)


def column_of(row):
    return jnp.broadcast_to(row, (128, row.shape[1])).T


def mix_head(query, key, value, row, entering=None):
    rows = query.shape[0]
    chunk = min(CHUNK, rows)
    column = column_of(row)
    causal = lax.broadcasted_iota(jnp.int32, (chunk, chunk), 0) >= lax.broadcasted_iota(
        jnp.int32, (chunk, chunk), 1
    )
    state = None if entering is None else entering.astype(F32)
    start_level = jnp.zeros((1, 1), F32)
    pieces = []
    for start in range(0, rows, chunk):
        stop = start + chunk
        q, k, v = query[start:stop], key[start:stop], value[start:stop]
        r, c = row[:, start:stop], column[start:stop]
        scores = lax.dot_general(q, k, (((1,), (1,)), ((), ())), preferred_element_type=F32)
        gap = jnp.where(causal, jnp.concatenate([c] * (chunk // 128), axis=1) - r, -1e30)
        weights = (scores * jnp.exp(gap)).astype(BF16)
        mixture = jnp.dot(weights, v, preferred_element_type=F32)
        if state is not None:
            scaled = (q.astype(F32) * jnp.exp(c - start_level)).astype(BF16)
            mixture = mixture + jnp.dot(scaled, state.astype(BF16), preferred_element_type=F32)
        pieces.append(mixture)
        if stop < rows:
            end = row[:, stop - 1 : stop]
            added = state_of(k, v, r, end)
            state = added if state is None else jnp.exp(end - start_level) * state + added
            start_level = end
    return pieces


def attend(first, heads, states_of, s_ref, levels_ref, gains_ref, *refs):
    z = s_ref[0]
    parts = 4
    streams, outs = refs[-3 - parts : -parts], refs[-parts:]
    states = refs[: -3 - parts]
    rows = levels_ref.shape[1]

    def step(*blocks):
        j = pl.program_id(0)
        for k in range(parts):
            home = lax.rem(z + k, parts)
            at = pl.ds(home * heads + first + j, 1)
            query, key, value = blocks[3 * k : 3 * k + 3]
            pieces = mix_head(query[...], key[...], value[...], levels_ref[at, :], states_of(states, k, home, j))
            size = pieces[0].shape[0]
            for n, piece in enumerate(pieces):
                blocks[3 * parts + k][n * size : (n + 1) * size, :] = norm(piece, gains_ref[at, :])

    specs = [
        pl.BlockSpec((rows, 128), lambda j, k=k: (0, lax.rem(z + k, parts) * heads + first + j)) for k in range(parts)
    ]
    pltpu.emit_pipeline(
        step,
        grid=(outs[0].shape[1] // 128,),
        in_specs=[spec for spec in specs for _ in range(3)],
        out_specs=[pl.BlockSpec((rows, 128), lambda j: (0, j))] * parts,
    )(*list(streams) * parts, *outs)


def own_parts(first, heads, s_ref, levels_ref, queries_ref, keys_ref, values_ref, *outs):
    z = s_ref[0]
    parts = len(outs)
    rows = levels_ref.shape[1]
    count = outs[0].shape[1] // 256

    def step(*blocks):
        j = pl.program_id(0)
        for k in range(parts):
            head = lax.rem(z + k, parts) * heads + first + j
            query, key, value = blocks[3 * k : 3 * k + 3]
            pieces = mix_head(query[...], key[...], value[...], levels_ref[pl.ds(head, 1), :])
            size = pieces[0].shape[0]
            for n, piece in enumerate(pieces):
                outs[k][n * size : (n + 1) * size, pl.ds(pl.multiple_of(j * 128, 128), 128)] = piece.astype(BF16)
            outs[k][:, pl.ds(pl.multiple_of((count + j) * 128, 128), 128)] = query[...]

    specs = [
        pl.BlockSpec((rows, 128), lambda j, k=k: (0, lax.rem(z + k, parts) * heads + first + j)) for k in range(parts)
    ]
    pltpu.emit_pipeline(step, grid=(count,), in_specs=[spec for spec in specs for _ in range(3)])(
        *[queries_ref, keys_ref, values_ref] * parts
    )


def finish(first, heads, s_ref, decay_ref, gains_ref, states_ref, *refs):
    parts = len(refs) // 2
    z = s_ref[0]
    rows, width = refs[parts].shape
    upper = lax.broadcasted_iota(jnp.int32, (rows, rows), 0) <= lax.broadcasted_iota(jnp.int32, (rows, rows), 1)
    upper = jnp.where(upper, 1.0, 0.0).astype(F32)
    for k in range(parts):
        c = lax.rem(z + parts - k, parts)
        levels = jnp.dot(
            decay_ref[:, pl.ds(pl.multiple_of(c * rows, 128), rows)], upper,
            precision=lax.Precision.HIGHEST, preferred_element_type=F32,
        )
        for j in range(width // 128):
            column = column_of(levels[first + j : first + j + 1, :])
            at = slice(j * 128, (j + 1) * 128)
            query = refs[k][:, width + j * 128 : width + (j + 1) * 128]
            scaled = (query.astype(F32) * jnp.exp(column)).astype(BF16)
            mixture = refs[k][:, at].astype(F32) + jnp.dot(scaled, states_ref[j, c], preferred_element_type=F32)
            refs[parts + k][:, at] = norm(mixture, gains_ref[pl.ds(z * heads + first + j, 1), :])


def place(first, parts, s_ref, *refs):
    pieces, out_ref, sems = refs[:parts], refs[-2], refs[-1]
    rows, width = pieces[0].shape
    copies = []
    for k in range(parts):
        source = lax.rem(s_ref[0] + parts - k, parts)
        copies.append(
            pltpu.make_async_copy(
                pieces[k],
                out_ref.at[pl.ds(pl.multiple_of(source * rows, rows), rows), pl.ds(first * 128, width)],
                sems.at[k],
            )
        )
    for copy in copies:
        copy.start()
    for copy in copies:
        copy.wait()


def local(queries, keys, values, log_decay, gain):
    heads, block = log_decay.shape
    parts, blocks = lax.axis_size("grp"), lax.axis_size("seq")
    rows = queries.shape[0]
    call = Calls(jnp.stack([lax.axis_index("grp"), lax.axis_index("seq")]).astype(jnp.int32))

    def shift(x, k):
        return lax.ppermute(x, "grp", [(i, (i + k) % parts) for i in range(parts)])

    def swap(x, axis, bit):
        return lax.ppermute(x, axis, [(i, i ^ bit) for i in range(lax.axis_size(axis))])

    starts = [sum(group[0] for group in GROUPS[:g]) for g in range(len(GROUPS))]
    packed = call(
        pack_decays, [log_decay, gain.reshape(heads, 128)], [shape(heads, rows + 256, dtype=F32)] * parts,
        cost=cost_us(8),
    )
    got = [packed[0]] + [shift(packed[k], k) for k in range(1, parts)]
    levels, totals, gains = call(
        unpack_decays, got,
        [shape(heads * parts, rows, dtype=F32), shape(heads * parts, 8, 128, dtype=F32), shape(heads * parts, 128, dtype=F32)],
        scratch=[pltpu.VMEM((heads * parts, rows), F32)],
    )

    def outputs(first, m, states, states_of):
        outs = call(
            functools.partial(attend, first, heads, states_of), [levels, gains, *states],
            [shape(rows, m * 128)] * parts,
            streams=[queries, keys, values],
            cost=cost_us(2.5 * m),
        )
        return first, [outs[0]] + [shift(outs[k], k) for k in range(1, parts)]

    def travel(first, m, done, calls, home_states):
        n = 2 * m

        def head_of(i, z, other):
            return (2 * (i // m) + lax.rem(z + other, 2)) * heads + first + i % m

        keep, send = call(
            functools.partial(half_states, first, heads), [levels],
            [shape(n, 128, 128)] * 2,
            streams=[keys, values],
            cost=cost_us(m),
        )
        got = swap(send, "grp", 1)
        yield
        pair, = call(functools.partial(pair_states, head_of), [keep, got, totals], [shape(n + done, 128, 128)])
        pair_got = swap(pair, "grp", 2)
        yield
        total, = call(functools.partial(block_states, head_of), [pair, pair_got, totals], [shape(n * 128 + log_rows(n), 128)])
        before = []
        bits = blocks.bit_length() - 1
        for bit in range(bits - 1):
            other = swap(total, "seq", 1 << bit)
            yield
            after, total = call(
                functools.partial(scan_blocks, bit), [total, other, *before],
                [shape(n, 136, 128, dtype=F32), shape(n * 128 + log_rows(n), 128)],
            )
            before = [after]
        other = swap(total, "seq", 1 << (bits - 1))
        yield
        rest = m - done
        own, send, *home = call(
            functools.partial(entering_states, first, heads, done, bits - 1),
            [total, other, *before, keep, got, pair, pair_got, totals],
            [shape(2 * rest, 128, 128)] * 2 + [shape(done, parts, 128, 128)] * (done > 0),
        )
        home_states.extend(home)
        states = [own, swap(send, "grp", 1)]
        yield
        start = 0
        for count in calls:

            def states_of(refs, k, home, j, start=start):
                return refs[k % 2][lax.div(home, 2) * rest + start + j]

            yield outputs(first + done + start, count, states, states_of)
            start += count

    def finished(first, done, arrived, home_states):
        parcels = call(
            functools.partial(own_parts, first, heads), [levels], [shape(rows, 2 * done * 128)] * parts,
            streams=[queries, keys, values],
            cost=cost_us(2 * done),
        )
        arrived += [parcels[0]] + [shift(parcels[k], k) for k in range(1, parts)]
        yield
        yield first, call(
            functools.partial(finish, first, heads), [log_decay, gains, *home_states, *arrived],
            [shape(rows, done * 128)] * parts,
        )

    home_states = [[] for _ in GROUPS]
    work = [travel(first, *group, home) for first, group, home in zip(starts, GROUPS, home_states)]
    arrived = [[] for _ in GROUPS]
    home_work = [
        finished(first, group[1], parcels, home)
        for first, group, parcels, home in zip(starts, GROUPS, arrived, home_states)
    ]
    pieces, out = [[] for _ in GROUPS], None
    for action, g, *rest in ORDER:
        g = int(g)
        if action in "kh":
            piece = next(work[g] if action == "k" else home_work[g])
            if piece is not None:
                pieces[g].append(piece)
        elif action == "d":
            call.after.append(arrived[g][int(rest[0])])
        elif action == "w":
            call.after.append(pieces[g][int(rest[0])][1][int(rest[1])])
        else:
            first, piece = pieces[g][int(rest[0])]
            out, = call(
                functools.partial(place, first, parts), [*piece, *([] if out is None else [out])],
                [shape(block, heads * 128)],
                out_specs=[anywhere()],
                scratch=[pltpu.SemaphoreType.DMA((parts,))],
                aliases={} if out is None else {parts: 0},
            )
    return out


def solution(mesh):
    parts, blocks = mesh.shape["grp"], mesh.shape["seq"]
    fits = parts == 4 and blocks >= 4 and blocks & (blocks - 1) == 0
    in_specs = (
        P(("seq", "grp"), None),
        P(("seq", "grp"), None),
        P(("seq", "grp"), None),
        P("grp", "seq"),
        P("grp"),
    )
    out_specs = P("seq", "grp")
    return jax.shard_map(
        local if fits else local_any, mesh=mesh, in_specs=in_specs, out_specs=out_specs, check_vma=False
    )
```
